512 devices in a mesh: dp: 32 (over z_hi, y), feat: 16 (over z_lo, x, core).
Axes of the slice: x: 4, y: 8, z: 8 (z_hi: 4, z_lo: 2; z = z_hi * 2 + z_lo), core: 2. Of those that a mesh axis runs over, the one named last changes fastest.
Arguments:
- first_view_outputs: bfloat16 [2048, 8192], P('dp', 'feat'), may hold values from -120 to 120
- second_view_outputs: bfloat16 [2048, 8192], P('feat', 'dp'), may hold values from -120 to 120
Outputs:
- first_view_gradient: bfloat16 [2048, 8192], P('dp', 'feat')
- second_view_gradient: bfloat16 [2048, 8192], P('feat', 'dp')
The draws below stay inside these ranges and needn't reach their ends.
All inputs are finite; a program needn't handle non-finite values.
Results may differ from the reference program's by a relative error of at most 0.033.
Values may be sent and summed in bfloat16 or wider, within the bound.
No kernel may reach another device: no remote copies, remote signals or barrier semaphores. Data moves between devices by JAX's collectives and lax.ppermute only.
A program may use at most 64 MiB of HBM per device.

```python
import math
import jax
import jax.numpy as jnp
from jax import lax

D = 8192
PAIRS = 2048
N_DP = 32
N_FEAT = 16


def shared_parts(key):
    sign_key, level_key, common_key = jax.random.split(key, 3)
    directions = D // 32
    sample_signs = (2 * jax.random.randint(sign_key, (PAIRS, directions), 0, 2) - 1).astype(jnp.float32)
    feature_levels = jax.random.randint(level_key, (directions, D), -3, 4).astype(jnp.float32)
    shared_sum = jnp.dot(sample_signs, feature_levels, precision=lax.Precision.HIGHEST)
    shared = jnp.clip(shared_sum * (1.0 / math.sqrt(4.0 * directions)), -5.0, 5.0)
    common = jnp.clip(jax.random.normal(common_key, (PAIRS, D), jnp.float32), -5.0, 5.0)
    return (shared, common)


def column_frame(key, low_scale, high_scale, offset):
    scale_key, shift_key = jax.random.split(key)
    scales = jnp.exp(jax.random.uniform(scale_key, (1, D), jnp.float32, math.log(low_scale), math.log(high_scale)))
    shifts = jax.random.uniform(shift_key, (1, D), jnp.float32, -offset, offset)
    return (scales, shifts)


def draw_first_view_outputs(key, part):
    shared, common = shared_parts(key)
    key = jax.random.fold_in(key, 11)
    scales, shifts = column_frame(key, 0.5, 4.0, 2.0)
    return (shifts + scales * (shared + common)).astype(jnp.bfloat16)


def draw_second_view_outputs(key, part):
    shared, common = shared_parts(key)
    key = jax.random.fold_in(key, 12)
    noise_key, frame_key = jax.random.split(key)
    noise_part = jnp.clip(jax.random.normal(noise_key, (PAIRS, D), jnp.float32), -5.0, 5.0)
    scales, shifts = column_frame(frame_key, 0.5, 4.0, 2.0)
    return (shifts + scales * (shared + 0.7 * common + 0.7 * noise_part)).astype(jnp.bfloat16)


def setup_inputs(seed: int = 0) -> dict:
    key_of = jax.random.split(jax.random.key(seed), 3)
    return {
        "first_view_outputs": draw_first_view_outputs(jax.random.fold_in(key_of[2], 71), 0),
        "second_view_outputs": draw_second_view_outputs(jax.random.fold_in(key_of[2], 71), 0),
    }


EPSILON = 1e-05
OFF_WEIGHT = 0.0051

def standardize_columns(values_in):
    values = values_in.astype(jnp.float32)
    center = lax.optimization_barrier(jnp.mean(values, axis=0))
    shifted = values - center
    spread = lax.optimization_barrier(jnp.mean(shifted * shifted, axis=0))
    inverse_scale = lax.rsqrt(spread + EPSILON)
    return (shifted * inverse_scale, inverse_scale)

def normalize_backward(normalized_gradient, standardized_values, inverse_scale):
    centering_term = lax.optimization_barrier(jnp.mean(normalized_gradient, axis=0))
    projection_term = lax.optimization_barrier(jnp.mean(normalized_gradient * standardized_values, axis=0))
    return ((normalized_gradient - centering_term - standardized_values * projection_term) * inverse_scale).astype(jnp.bfloat16)

def reference(first_view_outputs, second_view_outputs):
    standardized_first, inverse_deviation_first = standardize_columns(first_view_outputs)
    standardized_second, inverse_deviation_second = standardize_columns(second_view_outputs)
    normalized_first = standardized_first.astype(jnp.bfloat16)
    normalized_second = standardized_second.astype(jnp.bfloat16)
    row_width = D // N_FEAT
    col_width = D // N_DP

    def row_block(running, block_index):
        row_start = block_index * row_width
        left_cols = lax.dynamic_slice_in_dim(normalized_first, row_start, row_width, 1)
        correlation = lax.dot_general(left_cols, normalized_second, (((0,), (0,)), ((), ())), preferred_element_type=jnp.float32) / PAIRS
        row_ids = row_start + lax.broadcasted_iota(jnp.int32, (row_width, D), 0)
        col_ids = lax.broadcasted_iota(jnp.int32, (row_width, D), 1)
        grad_corr = jnp.where(row_ids == col_ids, 2.0 * (correlation - 1.0), 2.0 * OFF_WEIGHT * correlation).astype(jnp.bfloat16)

        def col_block(summed, column_index):
            col_start = column_index * col_width
            right_cols = lax.dynamic_slice_in_dim(normalized_second, col_start, col_width, 1)
            grad_tile = lax.dynamic_slice_in_dim(grad_corr, col_start, col_width, 1)
            partial_term = lax.dot_general(right_cols, grad_tile, (((1,), (1,)), ((), ())), preferred_element_type=jnp.float32)
            rounded = lax.optimization_barrier(partial_term.astype(jnp.bfloat16))
            return (summed + rounded.astype(jnp.float32), None)
        dnorm_block, _ = lax.scan(col_block, jnp.zeros((PAIRS, row_width), jnp.float32), jnp.arange(N_DP, dtype=jnp.int32))
        partial_b = jnp.dot(left_cols, grad_corr, preferred_element_type=jnp.float32)
        rounded_b = lax.optimization_barrier(partial_b.astype(jnp.bfloat16))
        return (running + rounded_b.astype(jnp.float32), dnorm_block)
    normalized_gradient_second, blocks = lax.scan(row_block, jnp.zeros((PAIRS, D), jnp.float32), jnp.arange(N_FEAT, dtype=jnp.int32))
    normalized_gradient_first = jnp.transpose(blocks, (1, 0, 2)).reshape(PAIRS, D)
    return (normalize_backward(normalized_gradient_first, standardized_first, inverse_deviation_first), normalize_backward(normalized_gradient_second, standardized_second, inverse_deviation_second))
```

```python
import jax
import jax.numpy as jnp
from jax import lax
from jax.sharding import Mesh, PartitionSpec as P

EPSILON = 1e-05
OFF_WEIGHT = 0.0051

SAMPLES = ("zh", "yk", "yl")
FEATURES = ("zl", "x", "core")
NEAR = ("yl", "zl", "x")


def exchange(values, axes):
    return lax.all_to_all(values, axes, 0, 0, tiled=True)


def statistics(values):
    wide = values.astype(jnp.float32)
    center = jnp.mean(wide, axis=0)
    shifted = wide - center
    inverse_scale = lax.rsqrt(jnp.mean(shifted * shifted, axis=0) + EPSILON)
    return (shifted * inverse_scale).astype(jnp.bfloat16), inverse_scale


def shards(first_view_outputs, second_view_outputs):
    rows_a, width_a = first_view_outputs.shape
    rows_b, width_b = second_view_outputs.shape
    n_dp = lax.axis_size(SAMPLES)
    n_near = lax.axis_size(NEAR)
    half = width_a // 2
    total_count = rows_a * n_dp
    parity = lax.axis_index("yl")

    gathered = exchange(
        jnp.broadcast_to(second_view_outputs, (n_near, rows_b, width_b)), NEAR
    )
    gathered = exchange(jnp.broadcast_to(gathered, (2, n_near, rows_b, width_b)), "core")
    second = (
        gathered.reshape(2, 2, n_near // 2, rows_b, width_b)
        .transpose(2, 0, 3, 1, 4)
        .reshape(total_count, 2 * width_b)
    )
    norm_second, inverse_second = statistics(second)

    halves = first_view_outputs.reshape(rows_a, 2, half).transpose(1, 0, 2)
    first = exchange(
        jnp.broadcast_to(halves, (n_dp // 2, 2, rows_a, half)).reshape(n_dp, rows_a, half),
        SAMPLES,
    ).reshape(total_count, half)
    norm_first, inverse_first = statistics(first)

    correlation = (
        lax.dot_general(
            norm_first,
            norm_second,
            (((0,), (0,)), ((), ())),
            preferred_element_type=jnp.float32,
        )
        / total_count
    )
    shape = correlation.shape
    row_ids = (
        lax.axis_index(FEATURES) * width_a
        + parity * half
        + lax.broadcasted_iota(jnp.int32, shape, 0)
    )
    col_ids = lax.axis_index(("zh", "yk")) * (2 * width_b) + lax.broadcasted_iota(
        jnp.int32, shape, 1
    )
    grad_tile = jnp.where(
        row_ids == col_ids, 2.0 * (correlation - 1.0), 2.0 * OFF_WEIGHT * correlation
    ).astype(jnp.bfloat16)
    grad_wide = grad_tile.astype(jnp.float32)
    weighted = grad_wide * correlation
    projection_first = jnp.sum(weighted, axis=1)
    projection_second = jnp.sum(weighted, axis=0)
    mean_first = jnp.mean(norm_first.astype(jnp.float32), axis=0)
    mean_second = jnp.mean(norm_second.astype(jnp.float32), axis=0)
    centering_first = jnp.sum(grad_wide * mean_second[None, :], axis=1)
    centering_second = jnp.sum(grad_wide * mean_first[:, None], axis=0)

    partial_second = (
        (
            jnp.dot(norm_first, grad_tile, preferred_element_type=jnp.float32)
            - centering_second
            - norm_second.astype(jnp.float32) * projection_second
        )
        * inverse_second
    ).astype(jnp.bfloat16)
    partial_first = (
        (
            lax.dot_general(
                norm_second,
                grad_tile,
                (((1,), (1,)), ((), ())),
                preferred_element_type=jnp.float32,
            )
            - centering_first
            - norm_first.astype(jnp.float32) * projection_first
        )
        * inverse_first
    ).astype(jnp.bfloat16)

    pieces = partial_second.reshape(n_near // 2, 2, rows_b, 2, width_b).transpose(1, 3, 0, 2, 4)
    pieces = exchange(pieces, "core")
    pieces = (pieces[0].astype(jnp.float32) + pieces[1].astype(jnp.float32)).astype(jnp.bfloat16)
    pieces = exchange(pieces.reshape(n_near, rows_b, width_b), NEAR)
    second_view_gradient = jnp.sum(pieces.astype(jnp.float32), axis=0).astype(jnp.bfloat16)

    parts = exchange(partial_first.reshape(n_dp, rows_a, half), SAMPLES)
    first_view_gradient = (
        jnp.sum(parts.reshape(n_dp // 2, 2, rows_a, half).astype(jnp.float32), axis=0)
        .astype(jnp.bfloat16)
        .transpose(1, 0, 2)
        .reshape(rows_a, width_a)
    )
    return first_view_gradient, second_view_gradient


def solution(mesh):
    fine = Mesh(
        mesh.devices.reshape(4, 4, 2, 2, 4, 2), ("zh", "yk", "yl", "zl", "x", "core")
    )
    specs = (P(SAMPLES, FEATURES), P(FEATURES, SAMPLES))
    return jax.shard_map(
        shards, mesh=fine, in_specs=specs, out_specs=specs, check_vma=False
    )
```

```python
import jax
import jax.numpy as jnp
from jax import lax
from jax.sharding import Mesh, PartitionSpec as P

EPSILON = 1e-05
OFF_WEIGHT = 0.0051

SAMPLES = ("zh", "yk", "yl")
FEATURES = ("zl", "x", "core")


def exchange(values, axes):
    return lax.all_to_all(values, axes, 0, 0, tiled=True)


def swap(values, axis):
    return lax.ppermute(values, axis, [(0, 1), (1, 0)])


def shift(values, distance):
    return lax.ppermute(values, "x", [(i, (i + distance) % 4) for i in range(4)])


def narrow_sum(*terms):
    return sum(term.astype(jnp.float32) for term in terms).astype(jnp.bfloat16)


def statistics(values):
    wide = values.astype(jnp.float32)
    center = jnp.mean(wide, axis=0)
    shifted = wide - center
    inverse_scale = lax.rsqrt(jnp.mean(shifted * shifted, axis=0) + EPSILON)
    return (shifted * inverse_scale).astype(jnp.bfloat16), inverse_scale


def shards(first_view_outputs, second_view_outputs):
    rows_a, width_a = first_view_outputs.shape
    rows_b, width_b = second_view_outputs.shape
    n_dp = lax.axis_size(SAMPLES)
    half = width_a // 2
    total_count = rows_a * n_dp
    parity = lax.axis_index("yl")

    grown = second_view_outputs
    for axis in ("yl", "zl"):
        other = swap(grown, axis)
        first_here = lax.axis_index(axis) == 0
        grown = jnp.stack(
            [jnp.where(first_here, grown, other), jnp.where(first_here, other, grown)]
        )
    ahead = [grown] + [shift(grown, -k) for k in (1, 2, 3)]
    grown = jnp.roll(jnp.stack(ahead), lax.axis_index("x"), axis=0)
    gathered = exchange(jnp.broadcast_to(grown, (2,) + grown.shape), "core")
    second = (
        gathered.reshape(2, 4, 2, 2, rows_b, width_b)
        .transpose(2, 1, 0, 4, 3, 5)
        .reshape(total_count, 2 * width_b)
    )
    norm_second, inverse_second = statistics(second)

    halves = first_view_outputs.reshape(rows_a, 2, half).transpose(1, 0, 2)
    first = exchange(
        jnp.broadcast_to(halves, (n_dp // 2, 2, rows_a, half)).reshape(n_dp, rows_a, half),
        SAMPLES,
    ).reshape(total_count, half)
    norm_first, inverse_first = statistics(first)

    correlation = (
        lax.dot_general(
            norm_first,
            norm_second,
            (((0,), (0,)), ((), ())),
            preferred_element_type=jnp.float32,
        )
        / total_count
    )
    shape = correlation.shape
    row_ids = (
        lax.axis_index(FEATURES) * width_a
        + parity * half
        + lax.broadcasted_iota(jnp.int32, shape, 0)
    )
    col_ids = lax.axis_index(("zh", "yk")) * (2 * width_b) + lax.broadcasted_iota(
        jnp.int32, shape, 1
    )
    grad_tile = jnp.where(
        row_ids == col_ids, 2.0 * (correlation - 1.0), 2.0 * OFF_WEIGHT * correlation
    ).astype(jnp.bfloat16)
    grad_wide = grad_tile.astype(jnp.float32)
    weighted = grad_wide * correlation
    projection_first = jnp.sum(weighted, axis=1)
    projection_second = jnp.sum(weighted, axis=0)
    mean_first = jnp.mean(norm_first.astype(jnp.float32), axis=0)
    mean_second = jnp.mean(norm_second.astype(jnp.float32), axis=0)
    centering_first = jnp.sum(grad_wide * mean_second[None, :], axis=1)
    centering_second = jnp.sum(grad_wide * mean_first[:, None], axis=0)

    partial_second = (
        (
            jnp.dot(norm_first, grad_tile, preferred_element_type=jnp.float32)
            - centering_second
            - norm_second.astype(jnp.float32) * projection_second
        )
        * inverse_second
    ).astype(jnp.bfloat16)
    partial_first = (
        (
            lax.dot_general(
                norm_second,
                grad_tile,
                (((1,), (1,)), ((), ())),
                preferred_element_type=jnp.float32,
            )
            - centering_first
            - norm_first.astype(jnp.float32) * projection_first
        )
        * inverse_first
    ).astype(jnp.bfloat16)

    pieces = partial_second.reshape(2, 4, 2, rows_b, 2, width_b).transpose(2, 1, 0, 4, 3, 5)
    pieces = exchange(pieces, "core")
    pieces = narrow_sum(pieces[0], pieces[1])
    here = lax.axis_index("x")
    moved = [shift(lax.dynamic_index_in_dim(pieces, (here + k) % 4, 0, False), k) for k in (1, 2, 3)]
    pieces = narrow_sum(lax.dynamic_index_in_dim(pieces, here, 0, False), *moved)
    for axis in ("zl", "yl"):
        here = lax.axis_index(axis)
        moved = swap(lax.dynamic_index_in_dim(pieces, 1 - here, 0, False), axis)
        pieces = narrow_sum(lax.dynamic_index_in_dim(pieces, here, 0, False), moved)
    second_view_gradient = pieces

    parts = exchange(partial_first.reshape(n_dp, rows_a, half), SAMPLES)
    first_view_gradient = (
        jnp.sum(parts.reshape(n_dp // 2, 2, rows_a, half).astype(jnp.float32), axis=0)
        .astype(jnp.bfloat16)
        .transpose(1, 0, 2)
        .reshape(rows_a, width_a)
    )
    return first_view_gradient, second_view_gradient


def solution(mesh):
    fine = Mesh(
        mesh.devices.reshape(4, 4, 2, 2, 4, 2), ("zh", "yk", "yl", "zl", "x", "core")
    )
    specs = (P(SAMPLES, FEATURES), P(FEATURES, SAMPLES))
    return jax.shard_map(
        shards, mesh=fine, in_specs=specs, out_specs=specs, check_vma=False
    )
```

```python
import jax
import jax.numpy as jnp
from jax import lax
from jax.sharding import Mesh, PartitionSpec as P

EPSILON = 1e-05
OFF_WEIGHT = 0.0051

SAMPLES = ("zh", "yk", "yl")
FEATURES = ("zl", "x", "core")


def exchange(values, axes):
    return lax.all_to_all(values, axes, 0, 0, tiled=True)


def swap(values, axis):
    return lax.ppermute(values, axis, [(0, 1), (1, 0)])


def shift(values, distance):
    return lax.ppermute(values, "x", [(i, (i + distance) % 4) for i in range(4)])


def narrow_sum(*terms):
    return sum(term.astype(jnp.float32) for term in terms).astype(jnp.bfloat16)


def statistics(values):
    wide = values.astype(jnp.float32)
    center = jnp.mean(wide, axis=0)
    shifted = wide - center
    inverse_scale = lax.rsqrt(jnp.mean(shifted * shifted, axis=0) + EPSILON)
    return (shifted * inverse_scale).astype(jnp.bfloat16), inverse_scale


def shards(first_view_outputs, second_view_outputs):
    rows_a, width_a = first_view_outputs.shape
    rows_b, width_b = second_view_outputs.shape
    n_dp = lax.axis_size(SAMPLES)
    half = width_a // 2
    total_count = rows_a * n_dp
    parity = lax.axis_index("yl")

    halves = first_view_outputs.reshape(rows_a, 2, half).transpose(1, 0, 2)
    first = exchange(
        jnp.broadcast_to(halves, (n_dp // 2, 2, rows_a, half)).reshape(n_dp, rows_a, half),
        SAMPLES,
    ).reshape(total_count, half)

    grown = second_view_outputs
    for axis in ("yl", "zl"):
        other = swap(grown, axis)
        first_here = lax.axis_index(axis) == 0
        grown = jnp.stack(
            [jnp.where(first_here, grown, other), jnp.where(first_here, other, grown)]
        )
    ahead = [grown] + [shift(grown, -k) for k in (1, 2, 3)]
    grown = jnp.roll(jnp.stack(ahead), lax.axis_index("x"), axis=0)
    first, grown = lax.optimization_barrier((first, grown))
    gathered = exchange(jnp.broadcast_to(grown, (2,) + grown.shape), "core")
    second = (
        gathered.reshape(2, 4, 2, 2, rows_b, width_b)
        .transpose(2, 1, 0, 4, 3, 5)
        .reshape(total_count, 2 * width_b)
    )
    norm_second, inverse_second = statistics(second)

    norm_first, inverse_first = statistics(first)

    correlation = (
        lax.dot_general(
            norm_first,
            norm_second,
            (((0,), (0,)), ((), ())),
            preferred_element_type=jnp.float32,
        )
        / total_count
    )
    shape = correlation.shape
    row_ids = (
        lax.axis_index(FEATURES) * width_a
        + parity * half
        + lax.broadcasted_iota(jnp.int32, shape, 0)
    )
    col_ids = lax.axis_index(("zh", "yk")) * (2 * width_b) + lax.broadcasted_iota(
        jnp.int32, shape, 1
    )
    grad_tile = jnp.where(
        row_ids == col_ids, 2.0 * (correlation - 1.0), 2.0 * OFF_WEIGHT * correlation
    ).astype(jnp.bfloat16)
    grad_wide = grad_tile.astype(jnp.float32)
    weighted = grad_wide * correlation
    projection_first = jnp.sum(weighted, axis=1)
    projection_second = jnp.sum(weighted, axis=0)
    mean_first = jnp.mean(norm_first.astype(jnp.float32), axis=0)
    mean_second = jnp.mean(norm_second.astype(jnp.float32), axis=0)
    centering_first = jnp.sum(grad_wide * mean_second[None, :], axis=1)
    centering_second = jnp.sum(grad_wide * mean_first[:, None], axis=0)

    partial_second = (
        (
            jnp.dot(norm_first, grad_tile, preferred_element_type=jnp.float32)
            - centering_second
            - norm_second.astype(jnp.float32) * projection_second
        )
        * inverse_second
    ).astype(jnp.bfloat16)
    partial_first = (
        (
            lax.dot_general(
                norm_second,
                grad_tile,
                (((1,), (1,)), ((), ())),
                preferred_element_type=jnp.float32,
            )
            - centering_first
            - norm_first.astype(jnp.float32) * projection_first
        )
        * inverse_first
    ).astype(jnp.bfloat16)

    pieces = partial_second.reshape(2, 4, 2, rows_b, 2, width_b).transpose(2, 1, 0, 4, 3, 5)
    pieces = exchange(pieces, "core")
    pieces = narrow_sum(pieces[0], pieces[1])
    here = lax.axis_index("x")
    moved = [shift(lax.dynamic_index_in_dim(pieces, (here + k) % 4, 0, False), k) for k in (1, 2, 3)]
    pieces = narrow_sum(lax.dynamic_index_in_dim(pieces, here, 0, False), *moved)
    for axis in ("zl", "yl"):
        here = lax.axis_index(axis)
        moved = swap(lax.dynamic_index_in_dim(pieces, 1 - here, 0, False), axis)
        pieces = narrow_sum(lax.dynamic_index_in_dim(pieces, here, 0, False), moved)
    second_view_gradient = pieces

    parts = exchange(partial_first.reshape(n_dp, rows_a, half), SAMPLES)
    first_view_gradient = (
        jnp.sum(parts.reshape(n_dp // 2, 2, rows_a, half).astype(jnp.float32), axis=0)
        .astype(jnp.bfloat16)
        .transpose(1, 0, 2)
        .reshape(rows_a, width_a)
    )
    return first_view_gradient, second_view_gradient


def solution(mesh):
    fine = Mesh(
        mesh.devices.reshape(4, 4, 2, 2, 4, 2), ("zh", "yk", "yl", "zl", "x", "core")
    )
    specs = (P(SAMPLES, FEATURES), P(FEATURES, SAMPLES))
    return jax.shard_map(
        shards, mesh=fine, in_specs=specs, out_specs=specs, check_vma=False
    )
```

```python
import functools

import jax
import jax.numpy as jnp
from jax import lax
from jax.experimental import pallas as pl
from jax.experimental.pallas import tpu as pltpu
from jax.sharding import Mesh, PartitionSpec as P

EPSILON = 1e-05
OFF_WEIGHT = 0.0051

SAMPLES = ("zh", "yk", "yl")
FEATURES = ("zl", "x", "core")
F32 = jnp.float32
BF16 = jnp.bfloat16
HIGHEST = lax.Precision.HIGHEST
VMEM_LIMIT = 28 * 1024 * 1024

BLOCK = 128
BLOCKS = 16


def exchange(values, axes):
    return lax.all_to_all(values, axes, 0, 0, tiled=True)


def near_swap(values, move):
    flip = 2 * (move % 2) + move // 2
    return lax.ppermute(values, ("yl", "zl"), [(i, i ^ flip) for i in range(4)])


def shift(values, distance):
    return lax.ppermute(values, "x", [(i, (i + distance) % 4) for i in range(4)])


def narrow_sum(*terms):
    return sum(term.astype(F32) for term in terms).astype(BF16)


def sample_row(place_ref, t):
    core = t // 8
    x = lax.rem(place_ref[0] + (t // 2) % 4, 4)
    zl = lax.rem(place_ref[1] + t % 2, 2)
    return pl.multiple_of(((zl * 4 + x) * 2 + core) * BLOCK, BLOCK)


def fold(values):
    return values.reshape(-1, 8, values.shape[-1]).sum(axis=0)


def tile_kernel(place_ref, first_ref, second_ref, moved_ref, na_ref, nb_ref, grad_ref, vectors_ref):
    count = BLOCK * BLOCKS
    width = first_ref.shape[1]

    def rows(t):
        return pl.ds(pl.multiple_of(t * BLOCK, BLOCK), BLOCK)

    def load(t):
        return (
            first_ref[rows(t), :].astype(F32),
            second_ref[t, 0].astype(F32),
            second_ref[t, 1].astype(F32),
        )

    zeros = (jnp.zeros((8, width), F32),) * 3

    def add_values(t, sums):
        return tuple(s + fold(v) for s, v in zip(sums, load(t)))

    sums = lax.fori_loop(0, BLOCKS, add_values, zeros)
    centers = [jnp.sum(s, axis=0, keepdims=True) / count for s in sums]

    def add_squares(t, sums):
        out = []
        for s, v, center in zip(sums, load(t), centers):
            shifted = v - center
            out.append(s + fold(shifted * shifted))
        return tuple(out)

    squares = lax.fori_loop(0, BLOCKS, add_squares, zeros)
    scales = [lax.rsqrt(jnp.sum(s, axis=0, keepdims=True) / count + EPSILON) for s in squares]

    def normalize(t, sums):
        a = first_ref[pl.ds(sample_row(place_ref, t), BLOCK), :].astype(F32)
        values = (a, second_ref[t, 0].astype(F32), second_ref[t, 1].astype(F32))
        out = []
        for i, (s, v, center, scale) in enumerate(zip(sums, values, centers, scales)):
            norm = ((v - center) * scale).astype(BF16)
            if i == 0:
                na_ref[rows(t), :] = norm
            else:
                nb_ref[rows(t), (i - 1) * width : i * width] = norm
            out.append(s + fold(norm.astype(F32)))
        return tuple(out)

    norm_sums = lax.fori_loop(0, BLOCKS, normalize, zeros)
    mean_first = norm_sums[0] / count
    mean_second = jnp.concatenate(norm_sums[1:], axis=1) / count

    correlation = (
        lax.dot_general(
            na_ref[...], nb_ref[...], (((0,), (0,)), ((), ())), preferred_element_type=F32
        )
        / count
    )
    row_ids = lax.broadcasted_iota(jnp.int32, correlation.shape, 0)
    col_ids = lax.broadcasted_iota(jnp.int32, correlation.shape, 1)
    grad = jnp.where(
        row_ids == col_ids + place_ref[2],
        2.0 * (correlation - 1.0),
        2.0 * OFF_WEIGHT * correlation,
    ).astype(BF16)
    grad_ref[...] = grad
    grad_wide = grad.astype(F32)
    weighted = grad_wide * correlation
    projection_second = jnp.sum(weighted, axis=0, keepdims=True)
    centering_second = jnp.sum(
        jnp.dot(mean_first, grad_wide, preferred_element_type=F32, precision=HIGHEST),
        axis=0,
        keepdims=True,
    )
    across = (((1,), (1,)), ((), ()))
    projection_first = lax.dot_general(
        jnp.ones((8, weighted.shape[1]), F32), weighted, across,
        preferred_element_type=F32, precision=HIGHEST,
    )
    centering_first = jnp.sum(
        lax.dot_general(
            mean_second, grad_wide, across, preferred_element_type=F32, precision=HIGHEST
        ),
        axis=0,
        keepdims=True,
    )
    vectors_ref[0:1, :] = centering_first
    vectors_ref[1:2, :] = projection_first[0:1]
    vectors_ref[2:3, :] = scales[0]
    scale_second = jnp.concatenate(scales[1:], axis=1)

    def back(t, carry):
        partial = jnp.dot(na_ref[rows(t), :], grad, preferred_element_type=F32)
        partial = (
            (partial - centering_second - nb_ref[rows(t), :].astype(F32) * projection_second)
            * scale_second
        ).astype(BF16)
        moved_ref[t, 0] = partial[:, :width]
        moved_ref[t, 1] = partial[:, width:]
        return carry

    lax.fori_loop(0, BLOCKS, back, 0)


def first_kernel(place_ref, na_ref, nb_ref, grad_ref, vectors_ref, out_ref):
    grad = grad_ref[...]
    centering, projection, scale = (vectors_ref[i : i + 1, :] for i in range(3))

    def back(t, carry):
        rows = pl.ds(pl.multiple_of(t * BLOCK, BLOCK), BLOCK)
        partial = lax.dot_general(
            nb_ref[rows, :], grad, (((1,), (1,)), ((), ())), preferred_element_type=F32
        )
        partial = (partial - centering - na_ref[rows, :].astype(F32) * projection) * scale
        out_ref[pl.ds(sample_row(place_ref, t), BLOCK), :] = partial.astype(BF16)
        return carry

    lax.fori_loop(0, BLOCKS, back, 0)


def call(kernel, outputs, flops, moved, *operands):
    spec = pl.BlockSpec(memory_space=pltpu.VMEM)
    return pl.pallas_call(
        kernel,
        out_shape=outputs,
        in_specs=[pl.BlockSpec(memory_space=pltpu.SMEM)] + [spec] * (len(operands) - 1),
        out_specs=jax.tree.map(lambda _: spec, outputs),
        compiler_params=pltpu.CompilerParams(vmem_limit_bytes=VMEM_LIMIT),
        cost_estimate=pl.CostEstimate(flops=flops, bytes_accessed=moved, transcendentals=0),
    )(*operands)


def shards(first_view_outputs, second_view_outputs):
    rows_a, width_a = first_view_outputs.shape
    rows_b, width_b = second_view_outputs.shape
    n_dp = lax.axis_size(SAMPLES)
    half = width_a // 2
    total_count = rows_a * n_dp
    shape = jax.ShapeDtypeStruct

    halves = jnp.stack([first_view_outputs[:, :half], first_view_outputs[:, half:]])
    first = exchange(
        jnp.broadcast_to(halves, (n_dp // 2, 2, rows_a, half)).reshape(n_dp, rows_a, half),
        SAMPLES,
    ).reshape(total_count, half)

    near = [second_view_outputs] + [near_swap(second_view_outputs, k) for k in (1, 2, 3)]
    near = jnp.stack(near)
    ahead = jnp.stack([near] + [shift(near, -k) for k in (1, 2, 3)])
    ahead = jnp.broadcast_to(ahead, (2,) + ahead.shape)
    first, ahead = lax.optimization_barrier((first, ahead))
    second = exchange(ahead, "core").reshape(BLOCKS, 2, rows_b, width_b)

    feat = lax.axis_index(FEATURES)
    pair = lax.axis_index(("zh", "yk"))
    place = jnp.stack(
        [
            lax.axis_index("x"),
            lax.axis_index("zl"),
            jnp.where(feat == pair, 0, 2 * width_a),
        ]
    ).astype(jnp.int32)
    flops = 2 * total_count * half * 2 * width_b
    moved, norm_first, norm_second, grad, vectors = call(
        tile_kernel,
        (
            shape((BLOCKS, 2, rows_b, width_b), BF16),
            shape((total_count, half), BF16),
            shape((total_count, 2 * width_b), BF16),
            shape((half, 2 * width_b), BF16),
            shape((8, half), F32),
        ),
        2 * flops, 8 << 20, place, first, second,
    )
    partial_first = call(
        first_kernel, shape((total_count, half), BF16), flops, 4 << 20,
        place, norm_first, norm_second, grad, vectors,
    )

    pieces = exchange(moved.reshape(2, 4, 4, rows_b, width_b), "core")
    pieces = narrow_sum(pieces[0], pieces[1])
    pieces = narrow_sum(pieces[0], *[shift(pieces[k], k) for k in (1, 2, 3)])
    second_view_gradient = narrow_sum(
        pieces[0], *[near_swap(pieces[k], k) for k in (1, 2, 3)]
    )

    parts = exchange(partial_first.reshape(n_dp, rows_a, half), SAMPLES)
    parts = jnp.sum(parts.reshape(n_dp // 2, 2, rows_a, half).astype(F32), axis=0).astype(BF16)
    first_view_gradient = jnp.concatenate([parts[0], parts[1]], axis=1)
    return first_view_gradient, second_view_gradient


def solution(mesh):
    fine = Mesh(
        mesh.devices.reshape(4, 4, 2, 2, 4, 2), ("zh", "yk", "yl", "zl", "x", "core")
    )
    specs = (P(SAMPLES, FEATURES), P(FEATURES, SAMPLES))
    return jax.shard_map(
        shards, mesh=fine, in_specs=specs, out_specs=specs, check_vma=False
    )
```

```python
import functools

import jax
import jax.numpy as jnp
from jax import lax
from jax.experimental import pallas as pl
from jax.experimental.pallas import tpu as pltpu
from jax.sharding import Mesh, PartitionSpec as P

EPSILON = 1e-05
OFF_WEIGHT = 0.0051

SAMPLES = ("zh", "yk", "yl")
FEATURES = ("zl", "x", "core")
F32 = jnp.float32
BF16 = jnp.bfloat16
HIGHEST = lax.Precision.HIGHEST
VMEM_LIMIT = 28 * 1024 * 1024

BLOCK = 128
BLOCKS = 16


def exchange(values, axes):
    return lax.all_to_all(values, axes, 0, 0, tiled=True)


def near_swap(values, move):
    flip = 2 * (move % 2) + move // 2
    return lax.ppermute(values, ("yl", "zl"), [(i, i ^ flip) for i in range(4)])


def shift(values, distance):
    return lax.ppermute(values, "x", [(i, (i + distance) % 4) for i in range(4)])


def narrow_sum(*terms):
    return sum(term.astype(F32) for term in terms).astype(BF16)


def sample_row(place_ref, t):
    core = t // 8
    x = lax.rem(place_ref[0] + (t // 2) % 4, 4)
    zl = lax.rem(place_ref[1] + t % 2, 2)
    return pl.multiple_of(((zl * 4 + x) * 2 + core) * BLOCK, BLOCK)


def fold(values):
    return values.reshape(-1, 8, values.shape[-1]).sum(axis=0)


def tile_kernel(place_ref, first_ref, second_ref, moved_ref, na_ref, nb_ref, grad_ref, vectors_ref):
    count = BLOCK * BLOCKS
    width = first_ref.shape[1]

    def rows(t):
        return pl.ds(pl.multiple_of(t * BLOCK, BLOCK), BLOCK)

    def load(t):
        return (
            first_ref[rows(t), :].astype(F32),
            second_ref[t, 0].astype(F32),
            second_ref[t, 1].astype(F32),
        )

    zeros = (jnp.zeros((8, width), F32),) * 3

    def add_values(t, sums):
        return tuple(s + fold(v) for s, v in zip(sums, load(t)))

    sums = lax.fori_loop(0, BLOCKS, add_values, zeros)
    centers = [jnp.sum(s, axis=0, keepdims=True) / count for s in sums]

    def add_squares(t, sums):
        out = []
        for s, v, center in zip(sums, load(t), centers):
            shifted = v - center
            out.append(s + fold(shifted * shifted))
        return tuple(out)

    squares = lax.fori_loop(0, BLOCKS, add_squares, zeros)
    scales = [lax.rsqrt(jnp.sum(s, axis=0, keepdims=True) / count + EPSILON) for s in squares]

    def normalize(t, sums):
        a = first_ref[pl.ds(sample_row(place_ref, t), BLOCK), :].astype(F32)
        values = (a, second_ref[t, 0].astype(F32), second_ref[t, 1].astype(F32))
        out = []
        for i, (s, v, center, scale) in enumerate(zip(sums, values, centers, scales)):
            norm = ((v - center) * scale).astype(BF16)
            if i == 0:
                na_ref[rows(t), :] = norm
            else:
                nb_ref[rows(t), (i - 1) * width : i * width] = norm
            out.append(s + fold(norm.astype(F32)))
        return tuple(out)

    norm_sums = lax.fori_loop(0, BLOCKS, normalize, zeros)
    mean_first = norm_sums[0] / count
    mean_second = jnp.concatenate(norm_sums[1:], axis=1) / count

    correlation = (
        lax.dot_general(
            na_ref[...], nb_ref[...], (((0,), (0,)), ((), ())), preferred_element_type=F32
        )
        / count
    )
    row_ids = lax.broadcasted_iota(jnp.int32, correlation.shape, 0)
    col_ids = lax.broadcasted_iota(jnp.int32, correlation.shape, 1)
    grad = jnp.where(
        row_ids == col_ids + place_ref[2],
        2.0 * (correlation - 1.0),
        2.0 * OFF_WEIGHT * correlation,
    ).astype(BF16)
    grad_ref[...] = grad
    grad_wide = grad.astype(F32)
    weighted = grad_wide * correlation
    projection_second = jnp.sum(weighted, axis=0, keepdims=True)
    centering_second = jnp.sum(
        jnp.dot(mean_first, grad_wide, preferred_element_type=F32, precision=HIGHEST),
        axis=0,
        keepdims=True,
    )
    across = (((1,), (1,)), ((), ()))
    projection_first = lax.dot_general(
        jnp.ones((8, weighted.shape[1]), F32), weighted, across,
        preferred_element_type=F32, precision=HIGHEST,
    )
    centering_first = jnp.sum(
        lax.dot_general(
            mean_second, grad_wide, across, preferred_element_type=F32, precision=HIGHEST
        ),
        axis=0,
        keepdims=True,
    )
    vectors_ref[0:1, :] = centering_first
    vectors_ref[1:2, :] = projection_first[0:1]
    vectors_ref[2:3, :] = scales[0]
    scale_second = jnp.concatenate(scales[1:], axis=1)

    def back(t, carry):
        partial = jnp.dot(na_ref[rows(t), :], grad, preferred_element_type=F32)
        partial = (
            (partial - centering_second - nb_ref[rows(t), :].astype(F32) * projection_second)
            * scale_second
        ).astype(BF16)
        moved_ref[t, 0] = partial[:, :width]
        moved_ref[t, 1] = partial[:, width:]
        return carry

    lax.fori_loop(0, BLOCKS, back, 0)


def first_kernel(place_ref, na_ref, nb_ref, grad_ref, vectors_ref, out_ref):
    grad = grad_ref[...]
    centering, projection, scale = (vectors_ref[i : i + 1, :] for i in range(3))

    def back(t, carry):
        rows = pl.ds(pl.multiple_of(t * BLOCK, BLOCK), BLOCK)
        partial = lax.dot_general(
            nb_ref[rows, :], grad, (((1,), (1,)), ((), ())), preferred_element_type=F32
        )
        partial = (partial - centering - na_ref[rows, :].astype(F32) * projection) * scale
        out_ref[pl.ds(sample_row(place_ref, t), BLOCK), :] = partial.astype(BF16)
        return carry

    lax.fori_loop(0, BLOCKS, back, 0)


def call(kernel, outputs, flops, moved, *operands):
    spec = pl.BlockSpec(memory_space=pltpu.VMEM)
    return pl.pallas_call(
        kernel,
        out_shape=outputs,
        in_specs=[pl.BlockSpec(memory_space=pltpu.SMEM)] + [spec] * (len(operands) - 1),
        out_specs=jax.tree.map(lambda _: spec, outputs),
        compiler_params=pltpu.CompilerParams(vmem_limit_bytes=VMEM_LIMIT),
        cost_estimate=pl.CostEstimate(flops=flops, bytes_accessed=moved, transcendentals=0),
    )(*operands)


def shards(first_view_outputs, second_view_outputs):
    rows_a, width_a = first_view_outputs.shape
    rows_b, width_b = second_view_outputs.shape
    n_dp = lax.axis_size(SAMPLES)
    half = width_a // 2
    total_count = rows_a * n_dp
    shape = jax.ShapeDtypeStruct

    near = [second_view_outputs] + [near_swap(second_view_outputs, k) for k in (1, 2, 3)]
    near = jnp.stack(near)
    halves = jnp.stack([first_view_outputs[:, :half], first_view_outputs[:, half:]])
    spread = jnp.broadcast_to(halves, (n_dp // 2, 2, rows_a, half)).reshape(n_dp, rows_a, half)
    near, spread = lax.optimization_barrier((near, spread))

    first = exchange(spread, SAMPLES).reshape(total_count, half)

    ahead = jnp.stack([near] + [shift(near, -k) for k in (1, 2, 3)])
    ahead = jnp.broadcast_to(ahead, (2,) + ahead.shape)
    first, ahead = lax.optimization_barrier((first, ahead))
    second = exchange(ahead, "core").reshape(BLOCKS, 2, rows_b, width_b)

    feat = lax.axis_index(FEATURES)
    pair = lax.axis_index(("zh", "yk"))
    place = jnp.stack(
        [
            lax.axis_index("x"),
            lax.axis_index("zl"),
            jnp.where(feat == pair, 0, 2 * width_a),
        ]
    ).astype(jnp.int32)
    flops = 2 * total_count * half * 2 * width_b
    moved, norm_first, norm_second, grad, vectors = call(
        tile_kernel,
        (
            shape((BLOCKS, 2, rows_b, width_b), BF16),
            shape((total_count, half), BF16),
            shape((total_count, 2 * width_b), BF16),
            shape((half, 2 * width_b), BF16),
            shape((8, half), F32),
        ),
        2 * flops, 8 << 20, place, first, second,
    )
    partial_first = call(
        first_kernel, shape((total_count, half), BF16), flops, 4 << 20,
        place, norm_first, norm_second, grad, vectors,
    )

    pieces = exchange(moved.reshape(2, 4, 4, rows_b, width_b), "core")
    pieces = narrow_sum(pieces[0], pieces[1])
    pieces = narrow_sum(pieces[0], *[shift(pieces[k], k) for k in (1, 2, 3)])
    second_view_gradient = narrow_sum(
        pieces[0], *[near_swap(pieces[k], k) for k in (1, 2, 3)]
    )

    parts = exchange(partial_first.reshape(n_dp, rows_a, half), SAMPLES)
    parts = jnp.sum(parts.reshape(n_dp // 2, 2, rows_a, half).astype(F32), axis=0).astype(BF16)
    first_view_gradient = jnp.concatenate([parts[0], parts[1]], axis=1)
    return first_view_gradient, second_view_gradient


def solution(mesh):
    fine = Mesh(
        mesh.devices.reshape(4, 4, 2, 2, 4, 2), ("zh", "yk", "yl", "zl", "x", "core")
    )
    specs = (P(SAMPLES, FEATURES), P(FEATURES, SAMPLES))
    return jax.shard_map(
        shards, mesh=fine, in_specs=specs, out_specs=specs, check_vma=False
    )
```

```python
import functools

import jax
import jax.numpy as jnp
from jax import lax
from jax.experimental import pallas as pl
from jax.experimental.pallas import tpu as pltpu
from jax.sharding import Mesh, PartitionSpec as P

EPSILON = 1e-05
OFF_WEIGHT = 0.0051

SAMPLES = ("zh", "yk", "yl")
FEATURES = ("zl", "x", "core")
F32 = jnp.float32
BF16 = jnp.bfloat16
HIGHEST = lax.Precision.HIGHEST
VMEM_LIMIT = 28 * 1024 * 1024

BLOCK = 128
BLOCKS = 16
CHUNK = 4


def exchange(values, axes):
    return lax.all_to_all(values, axes, 0, 0, tiled=True)


def near_swap(values, move):
    flip = 2 * (move % 2) + move // 2
    return lax.ppermute(values, ("yl", "zl"), [(i, i ^ flip) for i in range(4)])


def shift(values, distance):
    return lax.ppermute(values, "x", [(i, (i + distance) % 4) for i in range(4)])


def narrow_sum(*terms):
    return sum(term.astype(F32) for term in terms).astype(BF16)


def sample_row(place_ref, t):
    core = t // 8
    x = lax.rem(place_ref[0] + (t // 2) % 4, 4)
    zl = lax.rem(place_ref[1] + t % 2, 2)
    return pl.multiple_of(((zl * 4 + x) * 2 + core) * BLOCK, BLOCK)


def fold(values):
    return values.reshape(-1, 8, values.shape[-1]).sum(axis=0)


def column_statistics(load, blocks, count):
    pivot = jnp.mean(load(0), axis=0, keepdims=True)
    sums = jnp.zeros((8, pivot.shape[1]), F32)
    squares = sums
    for t in range(blocks):
        shifted = load(t) - pivot
        sums += fold(shifted)
        squares += fold(shifted * shifted)
    offset = jnp.sum(sums, axis=0, keepdims=True) / count
    spread = jnp.sum(squares, axis=0, keepdims=True) / count - offset * offset
    return pivot + offset, lax.rsqrt(jnp.maximum(spread, 0.0) + EPSILON)


def tile_kernel(
    place_ref, first_hbm, second_ref, moved_hbm, na_ref, nb_ref, grad_ref, vectors_ref,
    first_ref, moved_ref, load_sem, store_sems,
):
    count = BLOCK * BLOCKS
    width = first_ref.shape[1]
    load_first = pltpu.make_async_copy(first_hbm, first_ref, load_sem)
    load_first.start()

    scales = []
    means = []
    for i in range(2):
        load = lambda t: second_ref[t, i].astype(F32)
        center, scale = column_statistics(load, BLOCKS, count)
        sums = jnp.zeros((8, width), F32)
        for t in range(BLOCKS):
            norm = ((load(t) - center) * scale).astype(BF16)
            nb_ref[t * BLOCK : (t + 1) * BLOCK, i * width : (i + 1) * width] = norm
            sums += fold(norm.astype(F32))
        scales.append(scale)
        means.append(sums / count)
    scale_second = jnp.concatenate(scales, axis=1)
    mean_second = jnp.concatenate(means, axis=1)

    load_first.wait()
    load = lambda t: first_ref[t * BLOCK : (t + 1) * BLOCK, :].astype(F32)
    center, scale_first = column_statistics(load, BLOCKS, count)
    sums = jnp.zeros((8, width), F32)
    for t in range(BLOCKS):
        values = first_ref[pl.ds(sample_row(place_ref, t), BLOCK), :].astype(F32)
        norm = ((values - center) * scale_first).astype(BF16)
        na_ref[t * BLOCK : (t + 1) * BLOCK, :] = norm
        sums += fold(norm.astype(F32))
    mean_first = sums / count

    correlation = (
        lax.dot_general(
            na_ref[...], nb_ref[...], (((0,), (0,)), ((), ())), preferred_element_type=F32
        )
        / count
    )
    row_ids = lax.broadcasted_iota(jnp.int32, correlation.shape, 0)
    col_ids = lax.broadcasted_iota(jnp.int32, correlation.shape, 1)
    grad = jnp.where(
        row_ids == col_ids + place_ref[2],
        2.0 * (correlation - 1.0),
        2.0 * OFF_WEIGHT * correlation,
    ).astype(BF16)
    grad_ref[...] = grad
    grad_wide = grad.astype(F32)
    weighted = grad_wide * correlation
    projection_second = jnp.sum(weighted, axis=0, keepdims=True)
    centering_second = jnp.sum(
        jnp.dot(mean_first, grad_wide, preferred_element_type=F32, precision=HIGHEST),
        axis=0,
        keepdims=True,
    )
    stores = []
    for start in range(0, BLOCKS, CHUNK):
        some = slice(start * BLOCK, (start + CHUNK) * BLOCK)
        partial = jnp.dot(na_ref[some, :], grad, preferred_element_type=F32)
        partial = (
            (partial - centering_second - nb_ref[some, :].astype(F32) * projection_second)
            * scale_second
        ).astype(BF16)
        for i in range(2):
            moved_ref[start : start + CHUNK, i] = partial[:, i * width : (i + 1) * width].reshape(
                CHUNK, BLOCK, width
            )
        part = pl.ds(start, CHUNK)
        store = pltpu.make_async_copy(
            moved_ref.at[part], moved_hbm.at[part], store_sems.at[start // CHUNK]
        )
        store.start()
        stores.append(store)

    across = (((1,), (1,)), ((), ()))
    projection_first = lax.dot_general(
        jnp.ones((8, weighted.shape[1]), F32), weighted, across,
        preferred_element_type=F32, precision=HIGHEST,
    )
    centering_first = jnp.sum(
        lax.dot_general(
            mean_second, grad_wide, across, preferred_element_type=F32, precision=HIGHEST
        ),
        axis=0,
        keepdims=True,
    )
    vectors_ref[0:1, :] = centering_first
    vectors_ref[1:2, :] = projection_first[0:1]
    vectors_ref[2:3, :] = scale_first
    vectors_ref[3:8, :] = jnp.zeros((5, width), F32)
    for store in stores:
        store.wait()


def first_kernel(place_ref, na_ref, nb_ref, grad_ref, vectors_ref, out_hbm, out_ref, store_sems):
    grad = grad_ref[...]
    centering, projection, scale = (vectors_ref[i : i + 1, :] for i in range(3))
    stores = []
    for start in range(0, BLOCKS, CHUNK):
        some = slice(start * BLOCK, (start + CHUNK) * BLOCK)
        partial = lax.dot_general(
            nb_ref[some, :], grad, (((1,), (1,)), ((), ())), preferred_element_type=F32
        )
        partial = (partial - centering - na_ref[some, :].astype(F32) * projection) * scale
        out_ref[some, :] = partial.astype(BF16)
        for t in range(start, start + CHUNK):
            store = pltpu.make_async_copy(
                out_ref.at[pl.ds(t * BLOCK, BLOCK)],
                out_hbm.at[pl.ds(sample_row(place_ref, t), BLOCK)],
                store_sems.at[t],
            )
            store.start()
            stores.append(store)
    for store in stores:
        store.wait()


def local_compute(place, first, second):
    count, width = first.shape
    shape = jax.ShapeDtypeStruct
    smem, vmem, hbm = (pl.BlockSpec(memory_space=m) for m in (pltpu.SMEM, pltpu.VMEM, pltpu.HBM))
    params = pltpu.CompilerParams(vmem_limit_bytes=VMEM_LIMIT)
    flops = 2 * count * width * 2 * width
    first = pltpu.with_memory_space_constraint(first, pltpu.HBM)
    moved, *kept = pl.pallas_call(
        tile_kernel,
        out_shape=(
            pltpu.HBM(second.shape, BF16),
            shape((count, width), BF16),
            shape((count, 2 * width), BF16),
            shape((width, 2 * width), BF16),
            shape((8, width), F32),
        ),
        in_specs=[smem, hbm, vmem],
        out_specs=(hbm, vmem, vmem, vmem, vmem),
        scratch_shapes=[
            pltpu.VMEM((count, width), BF16),
            pltpu.VMEM(second.shape, BF16),
            pltpu.SemaphoreType.DMA,
            pltpu.SemaphoreType.DMA((BLOCKS // CHUNK,)),
        ],
        compiler_params=params,
        cost_estimate=pl.CostEstimate(flops=2 * flops, bytes_accessed=8 << 20, transcendentals=0),
    )(place, first, second)
    partial_first = pl.pallas_call(
        first_kernel,
        out_shape=pltpu.HBM((count, width), BF16),
        in_specs=[smem, vmem, vmem, vmem, vmem],
        out_specs=hbm,
        scratch_shapes=[pltpu.VMEM((count, width), BF16), pltpu.SemaphoreType.DMA((BLOCKS,))],
        compiler_params=params,
        cost_estimate=pl.CostEstimate(flops=flops, bytes_accessed=4 << 20, transcendentals=0),
    )(place, *kept)
    return moved, partial_first


def shards(first_view_outputs, second_view_outputs):
    rows_a, width_a = first_view_outputs.shape
    rows_b, width_b = second_view_outputs.shape
    n_dp = lax.axis_size(SAMPLES)
    half = width_a // 2
    total_count = rows_a * n_dp

    near = [near_swap(second_view_outputs, k) for k in (1, 2, 3)]
    halves = jnp.stack([first_view_outputs[:, :half], first_view_outputs[:, half:]])
    spread = jnp.broadcast_to(halves, (n_dp // 2, 2, rows_a, half)).reshape(n_dp, rows_a, half)
    near, spread = lax.optimization_barrier((near, spread))
    near = jnp.stack([second_view_outputs] + near)

    first = exchange(spread, SAMPLES).reshape(total_count, half)

    ahead = jnp.stack([near] + [shift(near, -k) for k in (1, 2, 3)])
    ahead = jnp.broadcast_to(ahead, (2,) + ahead.shape)
    first, ahead = lax.optimization_barrier((first, ahead))
    second = exchange(ahead, "core").reshape(BLOCKS, 2, rows_b, width_b)

    feat = lax.axis_index(FEATURES)
    pair = lax.axis_index(("zh", "yk"))
    place = jnp.stack(
        [
            lax.axis_index("x"),
            lax.axis_index("zl"),
            jnp.where(feat == pair, 0, 2 * width_a),
        ]
    ).astype(jnp.int32)
    moved, partial_first = local_compute(place, first, second)

    pieces = exchange(moved.reshape(2, 4, 4, rows_b, width_b), "core")
    pieces = narrow_sum(pieces[0], pieces[1])
    pieces = narrow_sum(pieces[0], *[shift(pieces[k], k) for k in (1, 2, 3)])
    second_view_gradient = narrow_sum(
        pieces[0], *[near_swap(pieces[k], k) for k in (1, 2, 3)]
    )

    parts = exchange(partial_first.reshape(n_dp, rows_a, half), SAMPLES)
    parts = jnp.sum(parts.reshape(n_dp // 2, 2, rows_a, half).astype(F32), axis=0).astype(BF16)
    first_view_gradient = jnp.concatenate([parts[0], parts[1]], axis=1)
    return first_view_gradient, second_view_gradient


def solution(mesh):
    fine = Mesh(
        mesh.devices.reshape(4, 4, 2, 2, 4, 2), ("zh", "yk", "yl", "zl", "x", "core")
    )
    specs = (P(SAMPLES, FEATURES), P(FEATURES, SAMPLES))
    return jax.shard_map(
        shards, mesh=fine, in_specs=specs, out_specs=specs, check_vma=False
    )
```

```python
import functools

import jax
import jax.numpy as jnp
from jax import lax
from jax.experimental import pallas as pl
from jax.experimental.pallas import tpu as pltpu
from jax.sharding import Mesh, PartitionSpec as P

EPSILON = 1e-05
OFF_WEIGHT = 0.0051

SAMPLES = ("zh", "yk", "yl")
FEATURES = ("zl", "x", "core")
F32 = jnp.float32
BF16 = jnp.bfloat16
HIGHEST = lax.Precision.HIGHEST
VMEM_LIMIT = 28 * 1024 * 1024

BLOCK = 128
BLOCKS = 16
CHUNK = 4


def exchange(values, axes):
    return lax.all_to_all(values, axes, 0, 0, tiled=True)


def near_swap(values, move):
    flip = 2 * (move % 2) + move // 2
    return lax.ppermute(values, ("yl", "zl"), [(i, i ^ flip) for i in range(4)])


def shift(values, distance):
    return lax.ppermute(values, "x", [(i, (i + distance) % 4) for i in range(4)])


def narrow_sum(*terms):
    return sum(term.astype(F32) for term in terms).astype(BF16)


def sample_row(place_ref, t):
    core = t // 8
    x = lax.rem(place_ref[0] + (t // 2) % 4, 4)
    zl = lax.rem(place_ref[1] + t % 2, 2)
    return pl.multiple_of(((zl * 4 + x) * 2 + core) * BLOCK, BLOCK)


def fold(values):
    return values.reshape(-1, 8, values.shape[-1]).sum(axis=0)


def column_statistics(load, blocks, count):
    pivot = jnp.mean(load(0), axis=0, keepdims=True)
    sums = jnp.zeros((8, pivot.shape[1]), F32)
    squares = sums
    for t in range(blocks):
        shifted = load(t) - pivot
        sums += fold(shifted)
        squares += fold(shifted * shifted)
    offset = jnp.sum(sums, axis=0, keepdims=True) / count
    spread = jnp.sum(squares, axis=0, keepdims=True) / count - offset * offset
    return pivot + offset, lax.rsqrt(jnp.maximum(spread, 0.0) + EPSILON)


def tile_kernel(
    place_ref, first_hbm, second_ref, moved_hbm, na_ref, nb_ref, grad_ref, vectors_ref,
    first_ref, moved_ref, load_sem, store_sems,
):
    count = BLOCK * BLOCKS
    width = first_ref.shape[1]
    load_first = pltpu.make_async_copy(first_hbm, first_ref, load_sem)
    load_first.start()

    scales = []
    means = []
    for i in range(2):
        load = lambda t: second_ref[t // 8, t % 2, i, (t // 2) % 4].astype(F32)
        center, scale = column_statistics(load, BLOCKS, count)
        sums = jnp.zeros((8, width), F32)
        for t in range(BLOCKS):
            norm = ((load(t) - center) * scale).astype(BF16)
            nb_ref[t * BLOCK : (t + 1) * BLOCK, i * width : (i + 1) * width] = norm
            sums += fold(norm.astype(F32))
        scales.append(scale)
        means.append(sums / count)
    scale_second = jnp.concatenate(scales, axis=1)
    mean_second = jnp.concatenate(means, axis=1)

    load_first.wait()
    load = lambda t: first_ref[t * BLOCK : (t + 1) * BLOCK, :].astype(F32)
    center, scale_first = column_statistics(load, BLOCKS, count)
    sums = jnp.zeros((8, width), F32)
    for t in range(BLOCKS):
        values = first_ref[pl.ds(sample_row(place_ref, t), BLOCK), :].astype(F32)
        norm = ((values - center) * scale_first).astype(BF16)
        na_ref[t * BLOCK : (t + 1) * BLOCK, :] = norm
        sums += fold(norm.astype(F32))
    mean_first = sums / count

    correlation = (
        lax.dot_general(
            na_ref[...], nb_ref[...], (((0,), (0,)), ((), ())), preferred_element_type=F32
        )
        / count
    )
    row_ids = lax.broadcasted_iota(jnp.int32, correlation.shape, 0)
    col_ids = lax.broadcasted_iota(jnp.int32, correlation.shape, 1)
    grad = jnp.where(
        row_ids == col_ids + place_ref[2],
        2.0 * (correlation - 1.0),
        2.0 * OFF_WEIGHT * correlation,
    ).astype(BF16)
    grad_ref[...] = grad
    grad_wide = grad.astype(F32)
    weighted = grad_wide * correlation
    projection_second = jnp.sum(weighted, axis=0, keepdims=True)
    centering_second = jnp.sum(
        jnp.dot(mean_first, grad_wide, preferred_element_type=F32, precision=HIGHEST),
        axis=0,
        keepdims=True,
    )
    stores = []
    for start in range(0, BLOCKS, CHUNK):
        some = slice(start * BLOCK, (start + CHUNK) * BLOCK)
        partial = jnp.dot(na_ref[some, :], grad, preferred_element_type=F32)
        partial = (
            (partial - centering_second - nb_ref[some, :].astype(F32) * projection_second)
            * scale_second
        ).astype(BF16)
        for i in range(2):
            moved_ref[start : start + CHUNK, i] = partial[:, i * width : (i + 1) * width].reshape(
                CHUNK, BLOCK, width
            )
        part = pl.ds(start, CHUNK)
        store = pltpu.make_async_copy(
            moved_ref.at[part], moved_hbm.at[part], store_sems.at[start // CHUNK]
        )
        store.start()
        stores.append(store)

    across = (((1,), (1,)), ((), ()))
    projection_first = lax.dot_general(
        jnp.ones((8, weighted.shape[1]), F32), weighted, across,
        preferred_element_type=F32, precision=HIGHEST,
    )
    centering_first = jnp.sum(
        lax.dot_general(
            mean_second, grad_wide, across, preferred_element_type=F32, precision=HIGHEST
        ),
        axis=0,
        keepdims=True,
    )
    vectors_ref[0:1, :] = centering_first
    vectors_ref[1:2, :] = projection_first[0:1]
    vectors_ref[2:3, :] = scale_first
    vectors_ref[3:8, :] = jnp.zeros((5, width), F32)
    for store in stores:
        store.wait()


def first_kernel(place_ref, na_ref, nb_ref, grad_ref, vectors_ref, out_hbm, out_ref, store_sems):
    grad = grad_ref[...]
    centering, projection, scale = (vectors_ref[i : i + 1, :] for i in range(3))
    stores = []
    for start in range(0, BLOCKS, CHUNK):
        some = slice(start * BLOCK, (start + CHUNK) * BLOCK)
        partial = lax.dot_general(
            nb_ref[some, :], grad, (((1,), (1,)), ((), ())), preferred_element_type=F32
        )
        partial = (partial - centering - na_ref[some, :].astype(F32) * projection) * scale
        out_ref[some, :] = partial.astype(BF16)
        for t in range(start, start + CHUNK):
            store = pltpu.make_async_copy(
                out_ref.at[pl.ds(t * BLOCK, BLOCK)],
                out_hbm.at[pl.ds(sample_row(place_ref, t), BLOCK)],
                store_sems.at[t],
            )
            store.start()
            stores.append(store)
    for store in stores:
        store.wait()


def local_compute(place, first, second):
    count, width = first.shape
    pieces = (BLOCKS, 2, BLOCK, width)
    shape = jax.ShapeDtypeStruct
    smem, vmem, hbm = (pl.BlockSpec(memory_space=m) for m in (pltpu.SMEM, pltpu.VMEM, pltpu.HBM))
    params = pltpu.CompilerParams(vmem_limit_bytes=VMEM_LIMIT)
    flops = 2 * count * width * 2 * width
    first = pltpu.with_memory_space_constraint(first, pltpu.HBM)
    moved, *kept = pl.pallas_call(
        tile_kernel,
        out_shape=(
            pltpu.HBM(pieces, BF16),
            shape((count, width), BF16),
            shape((count, 2 * width), BF16),
            shape((width, 2 * width), BF16),
            shape((8, width), F32),
        ),
        in_specs=[smem, hbm, vmem],
        out_specs=(hbm, vmem, vmem, vmem, vmem),
        scratch_shapes=[
            pltpu.VMEM((count, width), BF16),
            pltpu.VMEM(pieces, BF16),
            pltpu.SemaphoreType.DMA,
            pltpu.SemaphoreType.DMA((BLOCKS // CHUNK,)),
        ],
        compiler_params=params,
        cost_estimate=pl.CostEstimate(flops=2 * flops, bytes_accessed=8 << 20, transcendentals=0),
    )(place, first, second)
    partial_first = pl.pallas_call(
        first_kernel,
        out_shape=pltpu.HBM((count, width), BF16),
        in_specs=[smem, vmem, vmem, vmem, vmem],
        out_specs=hbm,
        scratch_shapes=[pltpu.VMEM((count, width), BF16), pltpu.SemaphoreType.DMA((BLOCKS,))],
        compiler_params=params,
        cost_estimate=pl.CostEstimate(flops=flops, bytes_accessed=4 << 20, transcendentals=0),
    )(place, *kept)
    return moved, partial_first


def shards(first_view_outputs, second_view_outputs):
    rows_a, width_a = first_view_outputs.shape
    rows_b, width_b = second_view_outputs.shape
    n_dp = lax.axis_size(SAMPLES)
    half = width_a // 2
    total_count = rows_a * n_dp

    halves = jnp.stack([first_view_outputs[:, :half], first_view_outputs[:, half:]])
    spread = jnp.broadcast_to(halves, (n_dp // 2, 2, rows_a, half)).reshape(n_dp, rows_a, half)
    first = exchange(spread, SAMPLES).reshape(total_count, half)

    ahead = jnp.stack([second_view_outputs] + [shift(second_view_outputs, -k) for k in (1, 2, 3)])
    near = jnp.stack([ahead] + [near_swap(ahead, k) for k in (1, 2, 3)])
    near = jnp.broadcast_to(near, (2,) + near.shape)
    first, near = lax.optimization_barrier((first, near))
    second = exchange(near, "core").reshape(2, 2, 2, 4, rows_b, width_b)

    feat = lax.axis_index(FEATURES)
    pair = lax.axis_index(("zh", "yk"))
    place = jnp.stack(
        [
            lax.axis_index("x"),
            lax.axis_index("zl"),
            jnp.where(feat == pair, 0, 2 * width_a),
        ]
    ).astype(jnp.int32)
    moved, partial_first = local_compute(place, first, second)

    pieces = exchange(moved.reshape(2, 4, 4, rows_b, width_b), "core")
    pieces = narrow_sum(pieces[0], pieces[1])
    pieces = narrow_sum(pieces[0], *[shift(pieces[k], k) for k in (1, 2, 3)])
    second_view_gradient = narrow_sum(
        pieces[0], *[near_swap(pieces[k], k) for k in (1, 2, 3)]
    )

    parts = exchange(partial_first.reshape(n_dp, rows_a, half), SAMPLES)
    parts = jnp.sum(parts.reshape(n_dp // 2, 2, rows_a, half).astype(F32), axis=0).astype(BF16)
    first_view_gradient = jnp.concatenate([parts[0], parts[1]], axis=1)
    return first_view_gradient, second_view_gradient


def solution(mesh):
    fine = Mesh(
        mesh.devices.reshape(4, 4, 2, 2, 4, 2), ("zh", "yk", "yl", "zl", "x", "core")
    )
    specs = (P(SAMPLES, FEATURES), P(FEATURES, SAMPLES))
    return jax.shard_map(
        shards, mesh=fine, in_specs=specs, out_specs=specs, check_vma=False
    )
```

```python
import functools

import jax
import jax.numpy as jnp
from jax import lax
from jax.experimental import pallas as pl
from jax.experimental.pallas import tpu as pltpu
from jax.sharding import Mesh, PartitionSpec as P

EPSILON = 1e-05
OFF_WEIGHT = 0.0051

SAMPLES = ("zh", "yk", "yl")
FEATURES = ("zl", "x", "core")
NEAR = ("yl", "zl")
F32 = jnp.float32
BF16 = jnp.bfloat16
HIGHEST = lax.Precision.HIGHEST
VMEM_LIMIT = 28 * 1024 * 1024

BLOCK = 128
BLOCKS = 16
CHUNK = 4


def exchange(values, axes):
    return lax.all_to_all(values, axes, 0, 0, tiled=True)


def near_swap(values, move):
    flip = 2 * (move % 2) + move // 2
    return lax.ppermute(values, NEAR, [(i, i ^ flip) for i in range(4)])


def shift(values, distance):
    return lax.ppermute(values, "x", [(i, (i + distance) % 4) for i in range(4)])


def narrow_sum(*terms):
    return sum(term.astype(F32) for term in terms).astype(BF16)


def sample_row(place_ref, t):
    core = t // 8
    x = lax.rem(place_ref[0] + (t // 2) % 4, 4)
    zl = lax.rem(place_ref[1] + t % 2, 2)
    return pl.multiple_of(((zl * 4 + x) * 2 + core) * BLOCK, BLOCK)


def fold(values):
    return values.reshape(-1, 8, values.shape[-1]).sum(axis=0)


def column_statistics(load, blocks, count):
    pivot = jnp.mean(load(0), axis=0, keepdims=True)
    sums = jnp.zeros((8, pivot.shape[1]), F32)
    squares = sums
    for t in range(blocks):
        shifted = load(t) - pivot
        sums += fold(shifted)
        squares += fold(shifted * shifted)
    offset = jnp.sum(sums, axis=0, keepdims=True) / count
    spread = jnp.sum(squares, axis=0, keepdims=True) / count - offset * offset
    return pivot + offset, lax.rsqrt(jnp.maximum(spread, 0.0) + EPSILON)


def tile_kernel(
    place_ref, first_hbm, second_ref, moved_hbm, out_hbm,
    first_ref, na_ref, nb_ref, moved_ref, out_ref, load_sem, moved_sems, out_sems,
):
    count = BLOCK * BLOCKS
    width = first_ref.shape[1]
    load_first = pltpu.make_async_copy(first_hbm, first_ref, load_sem)
    load_first.start()

    scales = []
    means = []
    for i in range(2):
        y = lax.rem(place_ref[3] + i, 2)
        load = lambda t: second_ref[
            t // 8, (t // 2) % 4, y, lax.rem(place_ref[1] + t % 2, 2)
        ].astype(F32)
        center, scale = column_statistics(load, BLOCKS, count)
        sums = jnp.zeros((8, width), F32)
        for t in range(BLOCKS):
            norm = ((load(t) - center) * scale).astype(BF16)
            nb_ref[t * BLOCK : (t + 1) * BLOCK, i * width : (i + 1) * width] = norm
            sums += fold(norm.astype(F32))
        scales.append(scale)
        means.append(sums / count)
    scale_second = jnp.concatenate(scales, axis=1)
    mean_second = jnp.concatenate(means, axis=1)

    load_first.wait()
    load = lambda t: first_ref[t * BLOCK : (t + 1) * BLOCK, :].astype(F32)
    center, scale_first = column_statistics(load, BLOCKS, count)
    sums = jnp.zeros((8, width), F32)
    for t in range(BLOCKS):
        values = first_ref[pl.ds(sample_row(place_ref, t), BLOCK), :].astype(F32)
        norm = ((values - center) * scale_first).astype(BF16)
        na_ref[t * BLOCK : (t + 1) * BLOCK, :] = norm
        sums += fold(norm.astype(F32))
    mean_first = sums / count

    correlation = (
        lax.dot_general(
            na_ref[...], nb_ref[...], (((0,), (0,)), ((), ())), preferred_element_type=F32
        )
        / count
    )
    row_ids = lax.broadcasted_iota(jnp.int32, correlation.shape, 0)
    col_ids = lax.broadcasted_iota(jnp.int32, correlation.shape, 1)
    grad = jnp.where(
        row_ids == col_ids + place_ref[2],
        2.0 * (correlation - 1.0),
        2.0 * OFF_WEIGHT * correlation,
    ).astype(BF16)
    grad_wide = grad.astype(F32)
    weighted = grad_wide * correlation
    projection_second = jnp.sum(weighted, axis=0, keepdims=True)
    centering_second = jnp.sum(
        jnp.dot(mean_first, grad_wide, preferred_element_type=F32, precision=HIGHEST),
        axis=0,
        keepdims=True,
    )
    stores = []
    for start in range(0, BLOCKS, CHUNK):
        some = slice(start * BLOCK, (start + CHUNK) * BLOCK)
        partial = jnp.dot(na_ref[some, :], grad, preferred_element_type=F32)
        partial = (
            (partial - centering_second - nb_ref[some, :].astype(F32) * projection_second)
            * scale_second
        ).astype(BF16)
        for i in range(2):
            moved_ref[start : start + CHUNK, i] = partial[:, i * width : (i + 1) * width].reshape(
                CHUNK, BLOCK, width
            )
        part = pl.ds(start, CHUNK)
        store = pltpu.make_async_copy(
            moved_ref.at[part], moved_hbm.at[part], moved_sems.at[start // CHUNK]
        )
        store.start()
        stores.append(store)

    across = (((1,), (1,)), ((), ()))
    projection_first = lax.dot_general(
        jnp.ones((8, weighted.shape[1]), F32), weighted, across,
        preferred_element_type=F32, precision=HIGHEST,
    )
    centering_first = jnp.sum(
        lax.dot_general(
            mean_second, grad_wide, across, preferred_element_type=F32, precision=HIGHEST
        ),
        axis=0,
        keepdims=True,
    )
    for start in range(0, BLOCKS, CHUNK):
        some = slice(start * BLOCK, (start + CHUNK) * BLOCK)
        partial = lax.dot_general(nb_ref[some, :], grad, across, preferred_element_type=F32)
        partial = (
            partial - centering_first - na_ref[some, :].astype(F32) * projection_first[0:1]
        ) * scale_first
        out_ref[some, :] = partial.astype(BF16)
        for t in range(start, start + CHUNK):
            store = pltpu.make_async_copy(
                out_ref.at[pl.ds(t * BLOCK, BLOCK)],
                out_hbm.at[pl.ds(sample_row(place_ref, t), BLOCK)],
                out_sems.at[t],
            )
            store.start()
            stores.append(store)
    for store in stores:
        store.wait()


def local_compute(place, first, second):
    count, width = first.shape
    pieces = (BLOCKS, 2, BLOCK, width)
    smem, vmem, hbm = (pl.BlockSpec(memory_space=m) for m in (pltpu.SMEM, pltpu.VMEM, pltpu.HBM))
    first = pltpu.with_memory_space_constraint(first, pltpu.HBM)
    return pl.pallas_call(
        tile_kernel,
        out_shape=(pltpu.HBM(pieces, BF16), pltpu.HBM((count, width), BF16)),
        in_specs=[smem, hbm, vmem],
        out_specs=(hbm, hbm),
        scratch_shapes=[
            pltpu.VMEM((count, width), BF16),
            pltpu.VMEM((count, width), BF16),
            pltpu.VMEM((count, 2 * width), BF16),
            pltpu.VMEM(pieces, BF16),
            pltpu.VMEM((count, width), BF16),
            pltpu.SemaphoreType.DMA,
            pltpu.SemaphoreType.DMA((BLOCKS // CHUNK,)),
            pltpu.SemaphoreType.DMA((BLOCKS,)),
        ],
        compiler_params=pltpu.CompilerParams(vmem_limit_bytes=VMEM_LIMIT),
        cost_estimate=pl.CostEstimate(
            flops=12 * count * width * width, bytes_accessed=6 << 20, transcendentals=0
        ),
    )(place, first, second)


def shards(first_view_outputs, second_view_outputs):
    rows_a, width_a = first_view_outputs.shape
    rows_b, width_b = second_view_outputs.shape
    n_dp = lax.axis_size(SAMPLES)
    half = width_a // 2
    total_count = rows_a * n_dp

    near = exchange(jnp.broadcast_to(second_view_outputs, (4, rows_b, width_b)), NEAR)
    halves = jnp.stack([first_view_outputs[:, :half], first_view_outputs[:, half:]])
    spread = jnp.broadcast_to(halves, (n_dp // 2, 2, rows_a, half)).reshape(n_dp, rows_a, half)
    near, spread = lax.optimization_barrier((near, spread))

    first = exchange(spread, SAMPLES).reshape(total_count, half)

    ahead = jnp.stack([near] + [shift(near, -k) for k in (1, 2, 3)])
    ahead = jnp.broadcast_to(ahead, (2,) + ahead.shape)
    first, ahead = lax.optimization_barrier((first, ahead))
    second = exchange(ahead, "core").reshape(2, 4, 2, 2, rows_b, width_b)

    feat = lax.axis_index(FEATURES)
    pair = lax.axis_index(("zh", "yk"))
    place = jnp.stack(
        [
            lax.axis_index("x"),
            lax.axis_index("zl"),
            jnp.where(feat == pair, 0, 2 * width_a),
            lax.axis_index("yl"),
        ]
    ).astype(jnp.int32)
    moved, partial_first = local_compute(place, first, second)

    pieces = exchange(moved.reshape(2, 4, 4, rows_b, width_b), "core")
    pieces = narrow_sum(pieces[0], pieces[1])
    pieces = narrow_sum(pieces[0], *[shift(pieces[k], k) for k in (1, 2, 3)])
    second_view_gradient = narrow_sum(
        pieces[0], *[near_swap(pieces[k], k) for k in (1, 2, 3)]
    )

    parts = exchange(partial_first.reshape(n_dp, rows_a, half), SAMPLES)
    parts = jnp.sum(parts.reshape(n_dp // 2, 2, rows_a, half).astype(F32), axis=0).astype(BF16)
    first_view_gradient = jnp.concatenate([parts[0], parts[1]], axis=1)
    return first_view_gradient, second_view_gradient


def solution(mesh):
    fine = Mesh(
        mesh.devices.reshape(4, 4, 2, 2, 4, 2), ("zh", "yk", "yl", "zl", "x", "core")
    )
    specs = (P(SAMPLES, FEATURES), P(FEATURES, SAMPLES))
    return jax.shard_map(
        shards, mesh=fine, in_specs=specs, out_specs=specs, check_vma=False
    )
```

```python
import functools

import jax
import jax.numpy as jnp
from jax import lax
from jax.experimental import pallas as pl
from jax.experimental.pallas import tpu as pltpu
from jax.sharding import Mesh, PartitionSpec as P

EPSILON = 1e-05
OFF_WEIGHT = 0.0051

SAMPLES = ("zh", "yk", "yl")
FEATURES = ("zl", "x", "core")
NEAR = ("yl", "zl")
F32 = jnp.float32
BF16 = jnp.bfloat16
HIGHEST = lax.Precision.HIGHEST
VMEM_LIMIT = 28 * 1024 * 1024

BLOCK = 128
BLOCKS = 16
CHUNK = 4


def exchange(values, axes):
    return lax.all_to_all(values, axes, 0, 0, tiled=True)


def near_swap(values, move):
    flip = 2 * (move % 2) + move // 2
    return lax.ppermute(values, NEAR, [(i, i ^ flip) for i in range(4)])


def shift(values, distance):
    return lax.ppermute(values, "x", [(i, (i + distance) % 4) for i in range(4)])


def narrow_sum(*terms):
    return sum(term.astype(F32) for term in terms).astype(BF16)


def sample_row(place_ref, t):
    core = t // 8
    x = lax.rem(place_ref[0] + (t // 2) % 4, 4)
    zl = lax.rem(place_ref[1] + t % 2, 2)
    return pl.multiple_of(((zl * 4 + x) * 2 + core) * BLOCK, BLOCK)


def fold(values):
    return values.reshape(-1, 8, values.shape[-1]).sum(axis=0)


def column_statistics(load, blocks, count):
    pivot = jnp.mean(load(0), axis=0, keepdims=True)
    sums = jnp.zeros((8, pivot.shape[1]), F32)
    squares = sums
    for t in range(blocks):
        shifted = load(t) - pivot
        sums += fold(shifted)
        squares += fold(shifted * shifted)
    offset = jnp.sum(sums, axis=0, keepdims=True) / count
    spread = jnp.sum(squares, axis=0, keepdims=True) / count - offset * offset
    return pivot + offset, lax.rsqrt(jnp.maximum(spread, 0.0) + EPSILON)


def tile_kernel(
    place_ref, first_hbm, second_ref, moved_ref, out_hbm,
    first_ref, na_ref, nb_ref, out_ref, load_sem, out_sems,
):
    count = BLOCK * BLOCKS
    width = first_ref.shape[1]
    load_first = pltpu.make_async_copy(first_hbm, first_ref, load_sem)
    load_first.start()

    scales = []
    means = []
    for i in range(2):
        y = lax.rem(place_ref[3] + i, 2)
        load = lambda t: second_ref[
            t // 8, (t // 2) % 4, y, lax.rem(place_ref[1] + t % 2, 2)
        ].astype(F32)
        center, scale = column_statistics(load, BLOCKS, count)
        sums = jnp.zeros((8, width), F32)
        for t in range(BLOCKS):
            norm = ((load(t) - center) * scale).astype(BF16)
            nb_ref[t * BLOCK : (t + 1) * BLOCK, i * width : (i + 1) * width] = norm
            sums += fold(norm.astype(F32))
        scales.append(scale)
        means.append(sums / count)
    scale_second = jnp.concatenate(scales, axis=1)
    mean_second = jnp.concatenate(means, axis=1)

    load_first.wait()
    load = lambda t: first_ref[t * BLOCK : (t + 1) * BLOCK, :].astype(F32)
    center, scale_first = column_statistics(load, BLOCKS, count)
    sums = jnp.zeros((8, width), F32)
    for t in range(BLOCKS):
        values = first_ref[pl.ds(sample_row(place_ref, t), BLOCK), :].astype(F32)
        norm = ((values - center) * scale_first).astype(BF16)
        na_ref[t * BLOCK : (t + 1) * BLOCK, :] = norm
        sums += fold(norm.astype(F32))
    mean_first = sums / count

    correlation = (
        lax.dot_general(
            na_ref[...], nb_ref[...], (((0,), (0,)), ((), ())), preferred_element_type=F32
        )
        / count
    )
    row_ids = lax.broadcasted_iota(jnp.int32, correlation.shape, 0)
    col_ids = lax.broadcasted_iota(jnp.int32, correlation.shape, 1)
    grad = jnp.where(
        row_ids == col_ids + place_ref[2],
        2.0 * (correlation - 1.0),
        2.0 * OFF_WEIGHT * correlation,
    ).astype(BF16)
    grad_wide = grad.astype(F32)
    weighted = grad_wide * correlation
    projection_second = jnp.sum(weighted, axis=0, keepdims=True)
    centering_second = jnp.sum(
        jnp.dot(mean_first, grad_wide, preferred_element_type=F32, precision=HIGHEST),
        axis=0,
        keepdims=True,
    )
    for start in range(0, BLOCKS, CHUNK):
        some = slice(start * BLOCK, (start + CHUNK) * BLOCK)
        partial = jnp.dot(na_ref[some, :], grad, preferred_element_type=F32)
        partial = (
            (partial - centering_second - nb_ref[some, :].astype(F32) * projection_second)
            * scale_second
        ).astype(BF16)
        for i in range(2):
            moved_ref[start : start + CHUNK, i] = partial[:, i * width : (i + 1) * width].reshape(
                CHUNK, BLOCK, width
            )

    across = (((1,), (1,)), ((), ()))
    projection_first = lax.dot_general(
        jnp.ones((8, weighted.shape[1]), F32), weighted, across,
        preferred_element_type=F32, precision=HIGHEST,
    )
    centering_first = jnp.sum(
        lax.dot_general(
            mean_second, grad_wide, across, preferred_element_type=F32, precision=HIGHEST
        ),
        axis=0,
        keepdims=True,
    )
    stores = []
    for start in range(0, BLOCKS, CHUNK):
        some = slice(start * BLOCK, (start + CHUNK) * BLOCK)
        partial = lax.dot_general(nb_ref[some, :], grad, across, preferred_element_type=F32)
        partial = (
            partial - centering_first - na_ref[some, :].astype(F32) * projection_first[0:1]
        ) * scale_first
        out_ref[some, :] = partial.astype(BF16)
        for t in range(start, start + CHUNK):
            store = pltpu.make_async_copy(
                out_ref.at[pl.ds(t * BLOCK, BLOCK)],
                out_hbm.at[pl.ds(sample_row(place_ref, t), BLOCK)],
                out_sems.at[t],
            )
            store.start()
            stores.append(store)
    for store in stores:
        store.wait()


def spread_kernel(values_ref, out_hbm, halves_ref, sems):
    width = halves_ref.shape[2]
    for i in range(2):
        halves_ref[i] = values_ref[:, i * width : (i + 1) * width]
    copies = [
        pltpu.make_async_copy(halves_ref, out_hbm.at[pl.ds(2 * i, 2)], sems.at[i])
        for i in range(out_hbm.shape[0] // 2)
    ]
    for copy in copies:
        copy.start()
    for copy in copies:
        copy.wait()


def spread_halves(values, copies):
    rows, width = values.shape
    shape = (rows, width // 2)
    return pl.pallas_call(
        spread_kernel,
        out_shape=pltpu.HBM((copies,) + shape, BF16),
        in_specs=[pl.BlockSpec(memory_space=pltpu.VMEM)],
        out_specs=pl.BlockSpec(memory_space=pltpu.HBM),
        scratch_shapes=[pltpu.VMEM((2,) + shape, BF16), pltpu.SemaphoreType.DMA((copies // 2,))],
        cost_estimate=pl.CostEstimate(flops=0, bytes_accessed=2 << 20, transcendentals=0),
    )(values)


def local_compute(place, first, second):
    count, width = first.shape
    pieces = (BLOCKS, 2, BLOCK, width)
    smem, vmem, hbm = (pl.BlockSpec(memory_space=m) for m in (pltpu.SMEM, pltpu.VMEM, pltpu.HBM))
    first = pltpu.with_memory_space_constraint(first, pltpu.HBM)
    return pl.pallas_call(
        tile_kernel,
        out_shape=(jax.ShapeDtypeStruct(pieces, BF16), pltpu.HBM((count, width), BF16)),
        in_specs=[smem, hbm, vmem],
        out_specs=(vmem, hbm),
        scratch_shapes=[
            pltpu.VMEM((count, width), BF16),
            pltpu.VMEM((count, width), BF16),
            pltpu.VMEM((count, 2 * width), BF16),
            pltpu.VMEM((count, width), BF16),
            pltpu.SemaphoreType.DMA,
            pltpu.SemaphoreType.DMA((BLOCKS,)),
        ],
        compiler_params=pltpu.CompilerParams(vmem_limit_bytes=VMEM_LIMIT),
        cost_estimate=pl.CostEstimate(
            flops=12 * count * width * width, bytes_accessed=6 << 20, transcendentals=0
        ),
    )(place, first, second)


def shards(first_view_outputs, second_view_outputs):
    rows_a, width_a = first_view_outputs.shape
    rows_b, width_b = second_view_outputs.shape
    n_dp = lax.axis_size(SAMPLES)
    half = width_a // 2
    total_count = rows_a * n_dp

    near = exchange(jnp.broadcast_to(second_view_outputs, (4, rows_b, width_b)), NEAR)
    spread = spread_halves(first_view_outputs, n_dp)
    near, spread = lax.optimization_barrier((near, spread))

    first = exchange(spread, SAMPLES).reshape(total_count, half)

    ahead = jnp.stack([near] + [shift(near, -k) for k in (1, 2, 3)])
    ahead = jnp.broadcast_to(ahead, (2,) + ahead.shape)
    first, ahead = lax.optimization_barrier((first, ahead))
    second = exchange(ahead, "core").reshape(2, 4, 2, 2, rows_b, width_b)

    feat = lax.axis_index(FEATURES)
    pair = lax.axis_index(("zh", "yk"))
    place = jnp.stack(
        [
            lax.axis_index("x"),
            lax.axis_index("zl"),
            jnp.where(feat == pair, 0, 2 * width_a),
            lax.axis_index("yl"),
        ]
    ).astype(jnp.int32)
    moved, partial_first = local_compute(place, first, second)

    pieces = exchange(moved.reshape(2, 4, 4, rows_b, width_b), "core")
    pieces = narrow_sum(pieces[0], pieces[1])
    pieces = narrow_sum(pieces[0], *[shift(pieces[k], k) for k in (1, 2, 3)])
    second_view_gradient = narrow_sum(
        pieces[0], *[near_swap(pieces[k], k) for k in (1, 2, 3)]
    )

    parts = exchange(partial_first.reshape(n_dp, rows_a, half), SAMPLES)
    parts = jnp.sum(parts.reshape(n_dp // 2, 2, rows_a, half).astype(F32), axis=0).astype(BF16)
    first_view_gradient = jnp.concatenate([parts[0], parts[1]], axis=1)
    return first_view_gradient, second_view_gradient


def solution(mesh):
    fine = Mesh(
        mesh.devices.reshape(4, 4, 2, 2, 4, 2), ("zh", "yk", "yl", "zl", "x", "core")
    )
    specs = (P(SAMPLES, FEATURES), P(FEATURES, SAMPLES))
    return jax.shard_map(
        shards, mesh=fine, in_specs=specs, out_specs=specs, check_vma=False
    )
```

```python
import functools

import jax
import jax.numpy as jnp
from jax import lax
from jax.experimental import pallas as pl
from jax.experimental.pallas import tpu as pltpu
from jax.sharding import Mesh, PartitionSpec as P

EPSILON = 1e-05
OFF_WEIGHT = 0.0051

SAMPLES = ("zh", "yk", "yl")
FEATURES = ("zl", "x", "core")
NEAR = ("yl", "zl")
F32 = jnp.float32
BF16 = jnp.bfloat16
VMEM_LIMIT = 28 * 1024 * 1024

BLOCK = 128
BLOCKS = 16
CHUNK = 4


def exchange(values, axes):
    return lax.all_to_all(values, axes, 0, 0, tiled=True)


def near_swap(values, move):
    flip = 2 * (move % 2) + move // 2
    return lax.ppermute(values, NEAR, [(i, i ^ flip) for i in range(4)])


def shift(values, distance):
    return lax.ppermute(values, "x", [(i, (i + distance) % 4) for i in range(4)])


def narrow_sum(*terms):
    return sum(term.astype(F32) for term in terms).astype(BF16)


def sample_row(place_ref, t):
    core = t // 8
    x = lax.rem(place_ref[0] + (t // 2) % 4, 4)
    zl = lax.rem(place_ref[1] + t % 2, 2)
    return pl.multiple_of(((zl * 4 + x) * 2 + core) * BLOCK, BLOCK)


def fold(values):
    return values.reshape(-1, 8, values.shape[-1]).sum(axis=0)


def split_rows(sums):
    row = jnp.sum(sums, axis=0, keepdims=True)
    rows = []
    for _ in range(3):
        rows.append(row.astype(BF16))
        row = row - rows[-1].astype(F32)
    return jnp.concatenate(rows + [jnp.zeros((13, row.shape[1]), BF16)], axis=0)


def column_statistics(load, blocks, count):
    pivot = jnp.mean(load(0), axis=0, keepdims=True)
    sums = jnp.zeros((8, pivot.shape[1]), F32)
    squares = sums
    for t in range(blocks):
        shifted = load(t) - pivot
        sums += fold(shifted)
        squares += fold(shifted * shifted)
    offset = jnp.sum(sums, axis=0, keepdims=True) / count
    spread = jnp.sum(squares, axis=0, keepdims=True) / count - offset * offset
    return pivot + offset, lax.rsqrt(jnp.maximum(spread, 0.0) + EPSILON)


def tile_kernel(
    place_ref, first_hbm, second_ref, moved_ref, out_hbm,
    first_ref, na_ref, nb_ref, out_ref, load_sem, out_sems,
):
    count = BLOCK * BLOCKS
    width = first_ref.shape[1]
    load_first = pltpu.make_async_copy(first_hbm, first_ref, load_sem)
    load_first.start()

    scales = []
    means = []
    for i in range(2):
        y = lax.rem(place_ref[3] + i, 2)
        load = lambda t: second_ref[
            t // 8, (t // 2) % 4, y, lax.rem(place_ref[1] + t % 2, 2)
        ].astype(F32)
        center, scale = column_statistics(load, BLOCKS, count)
        sums = jnp.zeros((8, width), F32)
        for t in range(BLOCKS):
            norm = ((load(t) - center) * scale).astype(BF16)
            nb_ref[t * BLOCK : (t + 1) * BLOCK, i * width : (i + 1) * width] = norm
            sums += fold(norm.astype(F32))
        scales.append(scale)
        means.append(sums / count)
    scale_second = jnp.concatenate(scales, axis=1)
    mean_second = jnp.concatenate(means, axis=1)

    load_first.wait()
    load = lambda t: first_ref[t * BLOCK : (t + 1) * BLOCK, :].astype(F32)
    center, scale_first = column_statistics(load, BLOCKS, count)
    sums = jnp.zeros((8, width), F32)
    for t in range(BLOCKS):
        values = first_ref[pl.ds(sample_row(place_ref, t), BLOCK), :].astype(F32)
        norm = ((values - center) * scale_first).astype(BF16)
        na_ref[t * BLOCK : (t + 1) * BLOCK, :] = norm
        sums += fold(norm.astype(F32))
    mean_first = sums / count

    correlation = (
        lax.dot_general(
            na_ref[...], nb_ref[...], (((0,), (0,)), ((), ())), preferred_element_type=F32
        )
        / count
    )
    row_ids = lax.broadcasted_iota(jnp.int32, correlation.shape, 0)
    col_ids = lax.broadcasted_iota(jnp.int32, correlation.shape, 1)
    grad = jnp.where(
        row_ids == col_ids + place_ref[2],
        2.0 * (correlation - 1.0),
        2.0 * OFF_WEIGHT * correlation,
    ).astype(BF16)
    grad_wide = grad.astype(F32)
    weighted = grad_wide * correlation
    projection_second = jnp.sum(weighted, axis=0, keepdims=True)
    centering_second = jnp.sum(
        jnp.dot(split_rows(mean_first), grad, preferred_element_type=F32), axis=0, keepdims=True
    )
    for start in range(0, BLOCKS, CHUNK):
        some = slice(start * BLOCK, (start + CHUNK) * BLOCK)
        partial = jnp.dot(na_ref[some, :], grad, preferred_element_type=F32)
        partial = (
            (partial - centering_second - nb_ref[some, :].astype(F32) * projection_second)
            * scale_second
        ).astype(BF16)
        for i in range(2):
            moved_ref[start : start + CHUNK, i] = partial[:, i * width : (i + 1) * width].reshape(
                CHUNK, BLOCK, width
            )

    across = (((1,), (1,)), ((), ()))
    lanes = 128
    folded = sum(weighted[:, i : i + lanes] for i in range(0, 2 * width, lanes))
    projection_first = jnp.sum(folded.T, axis=0, keepdims=True)
    centering_first = jnp.sum(
        lax.dot_general(split_rows(mean_second), grad, across, preferred_element_type=F32),
        axis=0,
        keepdims=True,
    )
    stores = []
    for start in range(0, BLOCKS, CHUNK):
        some = slice(start * BLOCK, (start + CHUNK) * BLOCK)
        partial = lax.dot_general(nb_ref[some, :], grad, across, preferred_element_type=F32)
        partial = (
            partial - centering_first - na_ref[some, :].astype(F32) * projection_first
        ) * scale_first
        out_ref[some, :] = partial.astype(BF16)
        for t in range(start, start + CHUNK):
            store = pltpu.make_async_copy(
                out_ref.at[pl.ds(t * BLOCK, BLOCK)],
                out_hbm.at[pl.ds(sample_row(place_ref, t), BLOCK)],
                out_sems.at[t],
            )
            store.start()
            stores.append(store)
    for store in stores:
        store.wait()


def spread_kernel(values_ref, out_hbm, halves_ref, sems):
    width = halves_ref.shape[2]
    for i in range(2):
        halves_ref[i] = values_ref[:, i * width : (i + 1) * width]
    copies = [
        pltpu.make_async_copy(halves_ref, out_hbm.at[pl.ds(2 * i, 2)], sems.at[i])
        for i in range(out_hbm.shape[0] // 2)
    ]
    for copy in copies:
        copy.start()
    for copy in copies:
        copy.wait()


def spread_halves(values, copies):
    rows, width = values.shape
    shape = (rows, width // 2)
    return pl.pallas_call(
        spread_kernel,
        out_shape=pltpu.HBM((copies,) + shape, BF16),
        in_specs=[pl.BlockSpec(memory_space=pltpu.VMEM)],
        out_specs=pl.BlockSpec(memory_space=pltpu.HBM),
        scratch_shapes=[pltpu.VMEM((2,) + shape, BF16), pltpu.SemaphoreType.DMA((copies // 2,))],
        cost_estimate=pl.CostEstimate(flops=0, bytes_accessed=2 << 20, transcendentals=0),
    )(values)


def local_compute(place, first, second):
    count, width = first.shape
    pieces = (BLOCKS, 2, BLOCK, width)
    smem, vmem, hbm = (pl.BlockSpec(memory_space=m) for m in (pltpu.SMEM, pltpu.VMEM, pltpu.HBM))
    first = pltpu.with_memory_space_constraint(first, pltpu.HBM)
    return pl.pallas_call(
        tile_kernel,
        out_shape=(jax.ShapeDtypeStruct(pieces, BF16), pltpu.HBM((count, width), BF16)),
        in_specs=[smem, hbm, vmem],
        out_specs=(vmem, hbm),
        scratch_shapes=[
            pltpu.VMEM((count, width), BF16),
            pltpu.VMEM((count, width), BF16),
            pltpu.VMEM((count, 2 * width), BF16),
            pltpu.VMEM((count, width), BF16),
            pltpu.SemaphoreType.DMA,
            pltpu.SemaphoreType.DMA((BLOCKS,)),
        ],
        compiler_params=pltpu.CompilerParams(vmem_limit_bytes=VMEM_LIMIT),
        cost_estimate=pl.CostEstimate(
            flops=12 * count * width * width, bytes_accessed=6 << 20, transcendentals=0
        ),
    )(place, first, second)


def shards(first_view_outputs, second_view_outputs):
    rows_a, width_a = first_view_outputs.shape
    rows_b, width_b = second_view_outputs.shape
    n_dp = lax.axis_size(SAMPLES)
    half = width_a // 2
    total_count = rows_a * n_dp

    near = exchange(jnp.broadcast_to(second_view_outputs, (4, rows_b, width_b)), NEAR)
    spread = spread_halves(first_view_outputs, n_dp)
    near, spread = lax.optimization_barrier((near, spread))

    first = exchange(spread, SAMPLES).reshape(total_count, half)

    ahead = jnp.stack([near] + [shift(near, -k) for k in (1, 2, 3)])
    ahead = jnp.broadcast_to(ahead, (2,) + ahead.shape)
    first, ahead = lax.optimization_barrier((first, ahead))
    second = exchange(ahead, "core").reshape(2, 4, 2, 2, rows_b, width_b)

    feat = lax.axis_index(FEATURES)
    pair = lax.axis_index(("zh", "yk"))
    place = jnp.stack(
        [
            lax.axis_index("x"),
            lax.axis_index("zl"),
            jnp.where(feat == pair, 0, 2 * width_a),
            lax.axis_index("yl"),
        ]
    ).astype(jnp.int32)
    moved, partial_first = local_compute(place, first, second)

    pieces = exchange(moved.reshape(2, 4, 4, rows_b, width_b), "core")
    pieces = narrow_sum(pieces[0], pieces[1])
    pieces = narrow_sum(pieces[0], *[shift(pieces[k], k) for k in (1, 2, 3)])
    pieces = [pieces[0]] + [near_swap(pieces[k], k) for k in (1, 2, 3)]

    parts = exchange(partial_first.reshape(n_dp, rows_a, half), SAMPLES)
    parts = jnp.sum(parts.reshape(n_dp // 2, 2, rows_a, half).astype(F32), axis=0).astype(BF16)
    first_view_gradient = jnp.concatenate([parts[0], parts[1]], axis=1)
    first_view_gradient, *pieces = lax.optimization_barrier([first_view_gradient] + pieces)
    return first_view_gradient, narrow_sum(*pieces)


def solution(mesh):
    fine = Mesh(
        mesh.devices.reshape(4, 4, 2, 2, 4, 2), ("zh", "yk", "yl", "zl", "x", "core")
    )
    specs = (P(SAMPLES, FEATURES), P(FEATURES, SAMPLES))
    return jax.shard_map(
        shards, mesh=fine, in_specs=specs, out_specs=specs, check_vma=False
    )
```

```python
import functools

import jax
import jax.numpy as jnp
from jax import lax
from jax.experimental import pallas as pl
from jax.experimental.pallas import tpu as pltpu
from jax.sharding import Mesh, PartitionSpec as P

EPSILON = 1e-05
OFF_WEIGHT = 0.0051

SAMPLES = ("zh", "yk", "yl")
FEATURES = ("zl", "x", "core")
NEAR = ("yl", "zl")
CHIPS = ("yl", "zl", "core")
F32 = jnp.float32
BF16 = jnp.bfloat16
VMEM_LIMIT = 28 * 1024 * 1024

BLOCK = 128
BLOCKS = 16
CHUNK = 4


def exchange(values, axes):
    return lax.all_to_all(values, axes, 0, 0, tiled=True)


def near_swap(values, move):
    flip = 2 * (move % 2) + move // 2
    return lax.ppermute(values, NEAR, [(i, i ^ flip) for i in range(4)])


def shift(values, distance):
    return lax.ppermute(values, "x", [(i, (i + distance) % 4) for i in range(4)])


def narrow_sum(*terms):
    return sum(term.astype(F32) for term in terms).astype(BF16)


def sample_block(place_ref, t):
    core = t // 8
    x = lax.rem(place_ref[0] + (t // 2) % 4, 4)
    zl = lax.rem(place_ref[1] + t % 2, 2)
    return (zl * 4 + x) * 2 + core


def fold(values):
    return values.reshape(-1, 8, values.shape[-1]).sum(axis=0)


def split_rows(sums):
    row = jnp.sum(sums, axis=0, keepdims=True)
    rows = []
    for _ in range(3):
        rows.append(row.astype(BF16))
        row = row - rows[-1].astype(F32)
    return jnp.concatenate(rows + [jnp.zeros((13, row.shape[1]), BF16)], axis=0)


def column_statistics(load, blocks, count):
    pivot = jnp.mean(load(0), axis=0, keepdims=True)
    sums = jnp.zeros((8, pivot.shape[1]), F32)
    squares = sums
    for t in range(blocks):
        shifted = load(t) - pivot
        sums += fold(shifted)
        squares += fold(shifted * shifted)
    offset = jnp.sum(sums, axis=0, keepdims=True) / count
    spread = jnp.sum(squares, axis=0, keepdims=True) / count - offset * offset
    return pivot + offset, lax.rsqrt(jnp.maximum(spread, 0.0) + EPSILON)


def tile_kernel(
    place_ref, first_ref, near_ref, right_ref, far_ref, left_ref, moved_ref, out_hbm,
    na_ref, nb_ref, out_ref, out_sems,
):
    count = BLOCK * BLOCKS
    width = first_ref.shape[2]
    pieces = BLOCK // first_ref.shape[1]

    def first_block(t):
        return first_ref[pl.ds(t * pieces, pieces)].reshape(BLOCK, width).astype(F32)

    ahead = (near_ref, right_ref, far_ref, left_ref)
    scales = []
    means = []
    for i in range(2):
        y = lax.rem(place_ref[3] + i, 2)
        load = lambda t: ahead[(t // 2) % 4][
            y, lax.rem(place_ref[1] + t % 2, 2), t // 8
        ].astype(F32)
        center, scale = column_statistics(load, BLOCKS, count)
        sums = jnp.zeros((8, width), F32)
        for t in range(BLOCKS):
            norm = ((load(t) - center) * scale).astype(BF16)
            nb_ref[t * BLOCK : (t + 1) * BLOCK, i * width : (i + 1) * width] = norm
            sums += fold(norm.astype(F32))
        scales.append(scale)
        means.append(sums / count)
    scale_second = jnp.concatenate(scales, axis=1)
    mean_second = jnp.concatenate(means, axis=1)

    center, scale_first = column_statistics(first_block, BLOCKS, count)
    sums = jnp.zeros((8, width), F32)
    for t in range(BLOCKS):
        norm = ((first_block(sample_block(place_ref, t)) - center) * scale_first).astype(BF16)
        na_ref[t * BLOCK : (t + 1) * BLOCK, :] = norm
        sums += fold(norm.astype(F32))
    mean_first = sums / count

    correlation = (
        lax.dot_general(
            na_ref[...], nb_ref[...], (((0,), (0,)), ((), ())), preferred_element_type=F32
        )
        / count
    )
    row_ids = lax.broadcasted_iota(jnp.int32, correlation.shape, 0)
    col_ids = lax.broadcasted_iota(jnp.int32, correlation.shape, 1)
    grad = jnp.where(
        row_ids == col_ids + place_ref[2],
        2.0 * (correlation - 1.0),
        2.0 * OFF_WEIGHT * correlation,
    ).astype(BF16)
    grad_wide = grad.astype(F32)
    weighted = grad_wide * correlation
    projection_second = jnp.sum(weighted, axis=0, keepdims=True)
    centering_second = jnp.sum(
        jnp.dot(split_rows(mean_first), grad, preferred_element_type=F32), axis=0, keepdims=True
    )
    for start in range(0, BLOCKS, CHUNK):
        some = slice(start * BLOCK, (start + CHUNK) * BLOCK)
        partial = jnp.dot(na_ref[some, :], grad, preferred_element_type=F32)
        partial = (
            (partial - centering_second - nb_ref[some, :].astype(F32) * projection_second)
            * scale_second
        ).astype(BF16)
        for i in range(2):
            moved_ref[start : start + CHUNK, i] = partial[:, i * width : (i + 1) * width].reshape(
                CHUNK, BLOCK, width
            )

    across = (((1,), (1,)), ((), ()))
    lanes = 128
    folded = sum(weighted[:, i : i + lanes] for i in range(0, 2 * width, lanes))
    projection_first = jnp.sum(folded.T, axis=0, keepdims=True)
    centering_first = jnp.sum(
        lax.dot_general(split_rows(mean_second), grad, across, preferred_element_type=F32),
        axis=0,
        keepdims=True,
    )
    stores = []
    for start in range(0, BLOCKS, CHUNK):
        some = slice(start * BLOCK, (start + CHUNK) * BLOCK)
        partial = lax.dot_general(nb_ref[some, :], grad, across, preferred_element_type=F32)
        partial = (
            partial - centering_first - na_ref[some, :].astype(F32) * projection_first
        ) * scale_first
        out_ref[some, :] = partial.astype(BF16)
        for t in range(start, start + CHUNK):
            row = pl.multiple_of(sample_block(place_ref, t) * BLOCK, BLOCK)
            store = pltpu.make_async_copy(
                out_ref.at[pl.ds(t * BLOCK, BLOCK)],
                out_hbm.at[pl.ds(row, BLOCK)],
                out_sems.at[t],
            )
            store.start()
            stores.append(store)
    for store in stores:
        store.wait()


def spread_kernel(values_ref, out_hbm, halves_ref, sems):
    width = halves_ref.shape[2]
    for i in range(2):
        halves_ref[i] = values_ref[:, i * width : (i + 1) * width]
    copies = [
        pltpu.make_async_copy(halves_ref, out_hbm.at[pl.ds(2 * i, 2)], sems.at[i])
        for i in range(out_hbm.shape[0] // 2)
    ]
    for copy in copies:
        copy.start()
    for copy in copies:
        copy.wait()


def spread_halves(values, copies):
    rows, width = values.shape
    shape = (rows, width // 2)
    return pl.pallas_call(
        spread_kernel,
        out_shape=pltpu.HBM((copies,) + shape, BF16),
        in_specs=[pl.BlockSpec(memory_space=pltpu.VMEM)],
        out_specs=pl.BlockSpec(memory_space=pltpu.HBM),
        scratch_shapes=[pltpu.VMEM((2,) + shape, BF16), pltpu.SemaphoreType.DMA((copies // 2,))],
        cost_estimate=pl.CostEstimate(flops=0, bytes_accessed=2 << 20, transcendentals=0),
    )(values)


def local_compute(place, first, second):
    count, width = first.shape[0] * first.shape[1], first.shape[2]
    pieces = (BLOCKS, 2, BLOCK, width)
    smem, vmem, hbm = (pl.BlockSpec(memory_space=m) for m in (pltpu.SMEM, pltpu.VMEM, pltpu.HBM))
    return pl.pallas_call(
        tile_kernel,
        out_shape=(jax.ShapeDtypeStruct(pieces, BF16), pltpu.HBM((count, width), BF16)),
        in_specs=[smem, vmem] + [vmem] * len(second),
        out_specs=(vmem, hbm),
        scratch_shapes=[
            pltpu.VMEM((count, width), BF16),
            pltpu.VMEM((count, 2 * width), BF16),
            pltpu.VMEM((count, width), BF16),
            pltpu.SemaphoreType.DMA((BLOCKS,)),
        ],
        compiler_params=pltpu.CompilerParams(vmem_limit_bytes=VMEM_LIMIT),
        cost_estimate=pl.CostEstimate(
            flops=12 * count * width * width, bytes_accessed=6 << 20, transcendentals=0
        ),
    )(place, first, *second)


def shards(first_view_outputs, second_view_outputs):
    rows_a, width_a = first_view_outputs.shape
    rows_b, width_b = second_view_outputs.shape
    n_dp = lax.axis_size(SAMPLES)
    half = width_a // 2

    near = exchange(jnp.broadcast_to(second_view_outputs, (8, rows_b, width_b)), CHIPS)
    spread = spread_halves(first_view_outputs, n_dp)
    near, spread = lax.optimization_barrier((near, spread))

    first = exchange(spread, SAMPLES)

    left, right = shift(near, 1), shift(near, -1)
    far = jnp.concatenate([shift(left[:4], 1), shift(right[4:], -1)])
    second = [v.reshape(2, 2, 2, rows_b, width_b) for v in (near, right, far, left)]

    feat = lax.axis_index(FEATURES)
    pair = lax.axis_index(("zh", "yk"))
    place = jnp.stack(
        [
            lax.axis_index("x"),
            lax.axis_index("zl"),
            jnp.where(feat == pair, 0, 2 * width_a),
            lax.axis_index("yl"),
        ]
    ).astype(jnp.int32)
    moved, partial_first = local_compute(place, first, second)

    pieces = exchange(moved.reshape(2, 4, 4, rows_b, width_b), "core")
    pieces = narrow_sum(pieces[0], pieces[1])
    pieces = narrow_sum(pieces[0], *[shift(pieces[k], k) for k in (1, 2, 3)])
    pieces = [pieces[0]] + [near_swap(pieces[k], k) for k in (1, 2, 3)]

    parts = exchange(partial_first.reshape(n_dp, rows_a, half), SAMPLES)
    parts = jnp.sum(parts.reshape(n_dp // 2, 2, rows_a, half).astype(F32), axis=0).astype(BF16)
    first_view_gradient = jnp.concatenate([parts[0], parts[1]], axis=1)
    first_view_gradient, *pieces = lax.optimization_barrier([first_view_gradient] + pieces)
    return first_view_gradient, narrow_sum(*pieces)


def solution(mesh):
    fine = Mesh(
        mesh.devices.reshape(4, 4, 2, 2, 4, 2), ("zh", "yk", "yl", "zl", "x", "core")
    )
    specs = (P(SAMPLES, FEATURES), P(FEATURES, SAMPLES))
    return jax.shard_map(
        shards, mesh=fine, in_specs=specs, out_specs=specs, check_vma=False
    )
```

```python
import functools

import jax
import jax.numpy as jnp
from jax import lax
from jax.experimental import pallas as pl
from jax.experimental.pallas import tpu as pltpu
from jax.sharding import Mesh, PartitionSpec as P

EPSILON = 1e-05
OFF_WEIGHT = 0.0051

SAMPLES = ("zh", "yk", "yl")
FEATURES = ("zl", "x", "core")
NEAR = ("yl", "zl")
F32 = jnp.float32
BF16 = jnp.bfloat16
VMEM_LIMIT = 28 * 1024 * 1024

BLOCK = 128
BLOCKS = 16
CHUNK = 4


def exchange(values, axes):
    return lax.all_to_all(values, axes, 0, 0, tiled=True)


def near_swap(values, move):
    flip = 2 * (move % 2) + move // 2
    return lax.ppermute(values, NEAR, [(i, i ^ flip) for i in range(4)])


def shift(values, distance):
    return lax.ppermute(values, "x", [(i, (i + distance) % 4) for i in range(4)])


def narrow_sum(*terms):
    return sum(term.astype(F32) for term in terms).astype(BF16)


def sample_block(place_ref, t):
    core = t // 8
    x = lax.rem(place_ref[0] + (t // 2) % 4, 4)
    zl = lax.rem(place_ref[1] + t % 2, 2)
    return (zl * 4 + x) * 2 + core


def fold(values):
    return values.reshape(-1, 8, values.shape[-1]).sum(axis=0)


def split_bf16(row):
    rows = []
    for _ in range(3):
        rows.append(row.astype(BF16))
        row = row - rows[-1].astype(F32)
    return rows


def split_rows(sums):
    rows = split_bf16(jnp.sum(sums, axis=0, keepdims=True))
    return jnp.concatenate(rows + [jnp.zeros((13, sums.shape[1]), BF16)], axis=0)


def column_moments(load, blocks, count):
    pivot = jnp.mean(load(0), axis=0, keepdims=True)
    sums = jnp.zeros((8, pivot.shape[1]), F32)
    squares = sums
    for t in range(blocks):
        shifted = load(t) - pivot
        sums += fold(shifted)
        squares += fold(shifted * shifted)
    sums = jnp.sum(sums, axis=0, keepdims=True)
    offset = sums / count
    return pivot + offset, jnp.sum(squares, axis=0, keepdims=True) - offset * sums


def half_kernel(*refs):
    block_refs, out_ref = refs[:-1], refs[-1]
    blocks = len(block_refs) * 2
    rows = []
    for y in range(2):
        load = lambda t: block_refs[t // 2][2 * y + t % 2].astype(F32)
        mean, squares = column_moments(load, blocks, blocks * BLOCK)
        rows += split_bf16(mean) + split_bf16(squares)
    rows.append(jnp.zeros((4, rows[0].shape[1]), BF16))
    for x, ref in enumerate(block_refs):
        for i in range(4):
            row = (x * 4 + i) * BLOCK
            out_ref[row : row + BLOCK, :] = ref[i]
    out_ref[len(block_refs) * 4 * BLOCK :, :] = jnp.concatenate(rows, axis=0)


def join_halves(first, second, y):
    first, second = first.astype(F32), second.astype(F32)

    def value(rows, i):
        return sum(rows[y * 6 + i * 3 + k : y * 6 + i * 3 + k + 1] for k in range(3))

    count = BLOCKS * BLOCK
    apart = value(first, 0) - value(second, 0)
    squares = value(first, 1) + value(second, 1) + apart * apart * (count / 4)
    mean = 0.5 * (value(first, 0) + value(second, 0))
    return mean, lax.rsqrt(jnp.maximum(squares, 0.0) / count + EPSILON)


def tile_kernel(
    place_ref, first_ref, second_ref, moved_ref, out_hbm,
    na_ref, nb_ref, out_ref, out_sems,
):
    count = BLOCK * BLOCKS
    width = first_ref.shape[2]
    pieces = BLOCK // first_ref.shape[1]

    def first_block(t):
        return first_ref[pl.ds(t * pieces, pieces)].reshape(BLOCK, width).astype(F32)

    statistics = [
        join_halves(*(second_ref[c, BLOCKS * BLOCK :, :] for c in range(2)), y)
        for y in range(2)
    ]
    scales = []
    means = []
    for i in range(2):
        y = lax.rem(place_ref[3] + i, 2)

        def load(t):
            block = (t // 2) % 4 * 4 + y * 2 + lax.rem(place_ref[1] + t % 2, 2)
            rows = pl.ds(pl.multiple_of(block * BLOCK, BLOCK), BLOCK)
            return second_ref[t // 8, rows, :].astype(F32)

        center, scale = (jnp.where(y == 0, u, v) for u, v in zip(*statistics))
        sums = jnp.zeros((8, width), F32)
        for t in range(BLOCKS):
            norm = ((load(t) - center) * scale).astype(BF16)
            nb_ref[t * BLOCK : (t + 1) * BLOCK, i * width : (i + 1) * width] = norm
            sums += fold(norm.astype(F32))
        scales.append(scale)
        means.append(sums / count)
    scale_second = jnp.concatenate(scales, axis=1)
    mean_second = jnp.concatenate(means, axis=1)

    center, squares = column_moments(first_block, BLOCKS, count)
    scale_first = lax.rsqrt(jnp.maximum(squares, 0.0) / count + EPSILON)
    sums = jnp.zeros((8, width), F32)
    for t in range(BLOCKS):
        norm = ((first_block(sample_block(place_ref, t)) - center) * scale_first).astype(BF16)
        na_ref[t * BLOCK : (t + 1) * BLOCK, :] = norm
        sums += fold(norm.astype(F32))
    mean_first = sums / count

    correlation = (
        lax.dot_general(
            na_ref[...], nb_ref[...], (((0,), (0,)), ((), ())), preferred_element_type=F32
        )
        / count
    )
    row_ids = lax.broadcasted_iota(jnp.int32, correlation.shape, 0)
    col_ids = lax.broadcasted_iota(jnp.int32, correlation.shape, 1)
    grad = jnp.where(
        row_ids == col_ids + place_ref[2],
        2.0 * (correlation - 1.0),
        2.0 * OFF_WEIGHT * correlation,
    ).astype(BF16)
    grad_wide = grad.astype(F32)
    weighted = grad_wide * correlation
    projection_second = jnp.sum(weighted, axis=0, keepdims=True)
    centering_second = jnp.sum(
        jnp.dot(split_rows(mean_first), grad, preferred_element_type=F32), axis=0, keepdims=True
    )
    for start in range(0, BLOCKS, CHUNK):
        some = slice(start * BLOCK, (start + CHUNK) * BLOCK)
        partial = jnp.dot(na_ref[some, :], grad, preferred_element_type=F32)
        partial = (
            (partial - centering_second - nb_ref[some, :].astype(F32) * projection_second)
            * scale_second
        ).astype(BF16)
        for i in range(2):
            moved_ref[start : start + CHUNK, i] = partial[:, i * width : (i + 1) * width].reshape(
                CHUNK, BLOCK, width
            )

    across = (((1,), (1,)), ((), ()))
    lanes = 128
    folded = sum(weighted[:, i : i + lanes] for i in range(0, 2 * width, lanes))
    projection_first = jnp.sum(folded.T, axis=0, keepdims=True)
    centering_first = jnp.sum(
        lax.dot_general(split_rows(mean_second), grad, across, preferred_element_type=F32),
        axis=0,
        keepdims=True,
    )
    stores = []
    for start in range(0, BLOCKS, CHUNK):
        some = slice(start * BLOCK, (start + CHUNK) * BLOCK)
        partial = lax.dot_general(nb_ref[some, :], grad, across, preferred_element_type=F32)
        partial = (
            partial - centering_first - na_ref[some, :].astype(F32) * projection_first
        ) * scale_first
        out_ref[some, :] = partial.astype(BF16)
        for t in range(start, start + CHUNK):
            row = pl.multiple_of(sample_block(place_ref, t) * BLOCK, BLOCK)
            store = pltpu.make_async_copy(
                out_ref.at[pl.ds(t * BLOCK, BLOCK)],
                out_hbm.at[pl.ds(row, BLOCK)],
                out_sems.at[t],
            )
            store.start()
            stores.append(store)
    for store in stores:
        store.wait()


def spread_kernel(values_ref, out_hbm, halves_ref, sems):
    width = halves_ref.shape[2]
    for i in range(2):
        halves_ref[i] = values_ref[:, i * width : (i + 1) * width]
    copies = [
        pltpu.make_async_copy(halves_ref, out_hbm.at[pl.ds(2 * i, 2)], sems.at[i])
        for i in range(out_hbm.shape[0] // 2)
    ]
    for copy in copies:
        copy.start()
    for copy in copies:
        copy.wait()


def spread_halves(values, copies):
    rows, width = values.shape
    shape = (rows, width // 2)
    return pl.pallas_call(
        spread_kernel,
        out_shape=pltpu.HBM((copies,) + shape, BF16),
        in_specs=[pl.BlockSpec(memory_space=pltpu.VMEM)],
        out_specs=pl.BlockSpec(memory_space=pltpu.HBM),
        scratch_shapes=[pltpu.VMEM((2,) + shape, BF16), pltpu.SemaphoreType.DMA((copies // 2,))],
        cost_estimate=pl.CostEstimate(flops=0, bytes_accessed=2 << 20, transcendentals=0),
    )(values)


def gather_half(parts):
    rows = len(parts) * 4 * BLOCK + 16
    spec = pl.BlockSpec(memory_space=pltpu.VMEM)
    return pl.pallas_call(
        half_kernel,
        out_shape=jax.ShapeDtypeStruct((rows, parts[0].shape[2]), BF16),
        in_specs=[spec] * len(parts),
        out_specs=spec,
        compiler_params=pltpu.CompilerParams(vmem_limit_bytes=VMEM_LIMIT),
        cost_estimate=pl.CostEstimate(flops=4 << 20, bytes_accessed=2 << 20, transcendentals=0),
    )(*parts)


def local_compute(place, first, second):
    count, width = first.shape[0] * first.shape[1], first.shape[2]
    pieces = (BLOCKS, 2, BLOCK, width)
    smem, vmem, hbm = (pl.BlockSpec(memory_space=m) for m in (pltpu.SMEM, pltpu.VMEM, pltpu.HBM))
    return pl.pallas_call(
        tile_kernel,
        out_shape=(jax.ShapeDtypeStruct(pieces, BF16), pltpu.HBM((count, width), BF16)),
        in_specs=[smem, vmem, vmem],
        out_specs=(vmem, hbm),
        scratch_shapes=[
            pltpu.VMEM((count, width), BF16),
            pltpu.VMEM((count, 2 * width), BF16),
            pltpu.VMEM((count, width), BF16),
            pltpu.SemaphoreType.DMA((BLOCKS,)),
        ],
        compiler_params=pltpu.CompilerParams(vmem_limit_bytes=VMEM_LIMIT),
        cost_estimate=pl.CostEstimate(
            flops=12 * count * width * width, bytes_accessed=6 << 20, transcendentals=0
        ),
    )(place, first, second)


def shards(first_view_outputs, second_view_outputs):
    rows_a, width_a = first_view_outputs.shape
    rows_b, width_b = second_view_outputs.shape
    n_dp = lax.axis_size(SAMPLES)
    half = width_a // 2

    near = exchange(jnp.broadcast_to(second_view_outputs, (4, rows_b, width_b)), NEAR)
    spread = spread_halves(first_view_outputs, n_dp)
    near, spread = lax.optimization_barrier((near, spread))

    first = exchange(spread, SAMPLES)

    own = gather_half([near] + [shift(near, -k) for k in (1, 2, 3)])
    own = jnp.broadcast_to(own, (2,) + own.shape)
    first, own = lax.optimization_barrier((first, own))
    second = exchange(own, "core")

    feat = lax.axis_index(FEATURES)
    pair = lax.axis_index(("zh", "yk"))
    place = jnp.stack(
        [
            lax.axis_index("x"),
            lax.axis_index("zl"),
            jnp.where(feat == pair, 0, 2 * width_a),
            lax.axis_index("yl"),
        ]
    ).astype(jnp.int32)
    moved, partial_first = local_compute(place, first, second)

    pieces = exchange(moved.reshape(2, 4, 4, rows_b, width_b), "core")
    pieces = narrow_sum(pieces[0], pieces[1])
    pieces = narrow_sum(pieces[0], *[shift(pieces[k], k) for k in (1, 2, 3)])
    pieces = [pieces[0]] + [near_swap(pieces[k], k) for k in (1, 2, 3)]

    parts = exchange(partial_first.reshape(n_dp, rows_a, half), SAMPLES)
    parts = jnp.sum(parts.reshape(n_dp // 2, 2, rows_a, half).astype(F32), axis=0).astype(BF16)
    first_view_gradient = jnp.concatenate([parts[0], parts[1]], axis=1)
    first_view_gradient, *pieces = lax.optimization_barrier([first_view_gradient] + pieces)
    return first_view_gradient, narrow_sum(*pieces)


def solution(mesh):
    fine = Mesh(
        mesh.devices.reshape(4, 4, 2, 2, 4, 2), ("zh", "yk", "yl", "zl", "x", "core")
    )
    specs = (P(SAMPLES, FEATURES), P(FEATURES, SAMPLES))
    return jax.shard_map(
        shards, mesh=fine, in_specs=specs, out_specs=specs, check_vma=False
    )
```

```python
import functools

import jax
import jax.numpy as jnp
from jax import lax
from jax.experimental import pallas as pl
from jax.experimental.pallas import tpu as pltpu
from jax.sharding import Mesh, PartitionSpec as P

EPSILON = 1e-05
OFF_WEIGHT = 0.0051

SAMPLES = ("zh", "yk", "yl")
FEATURES = ("zl", "x", "core")
NEAR = ("yl", "zl")
F32 = jnp.float32
BF16 = jnp.bfloat16
VMEM_LIMIT = 28 * 1024 * 1024

BLOCK = 128
BLOCKS = 16
CHUNK = 4


def exchange(values, axes):
    return lax.all_to_all(values, axes, 0, 0, tiled=True)


def near_swap(values, move):
    flip = 2 * (move % 2) + move // 2
    return lax.ppermute(values, NEAR, [(i, i ^ flip) for i in range(4)])


def shift(values, distance):
    return lax.ppermute(values, "x", [(i, (i + distance) % 4) for i in range(4)])


def narrow_sum(*terms):
    return sum(term.astype(F32) for term in terms).astype(BF16)


def sample_block(place_ref, t):
    core = t // 8
    x = lax.rem(place_ref[0] + (t // 2) % 4, 4)
    zl = lax.rem(place_ref[1] + t % 2, 2)
    return (zl * 4 + x) * 2 + core


def fold(values):
    return values.reshape(-1, 8, values.shape[-1]).sum(axis=0)


def split_bf16(row):
    rows = []
    for _ in range(3):
        rows.append(row.astype(BF16))
        row = row - rows[-1].astype(F32)
    return rows


def split_rows(sums):
    rows = split_bf16(jnp.sum(sums, axis=0, keepdims=True))
    return jnp.concatenate(rows + [jnp.zeros((13, sums.shape[1]), BF16)], axis=0)


def column_moments(load, blocks, count):
    pivot = jnp.mean(load(0), axis=0, keepdims=True)
    sums = jnp.zeros((8, pivot.shape[1]), F32)
    squares = sums
    for t in range(blocks):
        shifted = load(t) - pivot
        sums += fold(shifted)
        squares += fold(shifted * shifted)
    sums = jnp.sum(sums, axis=0, keepdims=True)
    offset = sums / count
    return pivot + offset, jnp.sum(squares, axis=0, keepdims=True) - offset * sums


def half_kernel(*refs):
    block_refs, out_ref = refs[:-1], refs[-1]
    blocks = len(block_refs) * 2
    rows = []
    for y in range(2):
        load = lambda t: block_refs[t // 2][2 * y + t % 2].astype(F32)
        mean, squares = column_moments(load, blocks, blocks * BLOCK)
        rows += split_bf16(mean) + split_bf16(squares)
    rows.append(jnp.zeros((4, rows[0].shape[1]), BF16))
    for x, ref in enumerate(block_refs):
        for i in range(4):
            row = (x * 4 + i) * BLOCK
            out_ref[row : row + BLOCK, :] = ref[i]
    out_ref[len(block_refs) * 4 * BLOCK :, :] = jnp.concatenate(rows, axis=0)


def join_halves(first, second, y):
    first, second = first.astype(F32), second.astype(F32)

    def value(rows, i):
        return sum(rows[y * 6 + i * 3 + k : y * 6 + i * 3 + k + 1] for k in range(3))

    count = BLOCKS * BLOCK
    apart = value(first, 0) - value(second, 0)
    squares = value(first, 1) + value(second, 1) + apart * apart * (count / 4)
    mean = 0.5 * (value(first, 0) + value(second, 0))
    return mean, lax.rsqrt(jnp.maximum(squares, 0.0) / count + EPSILON)


def tile_kernel(
    place_ref, first_ref, second_ref, moved_ref, out_hbm,
    na_ref, nb_ref, out_ref, out_sems,
):
    count = BLOCK * BLOCKS
    width = first_ref.shape[2]
    pieces = BLOCK // first_ref.shape[1]

    def first_block(t):
        return first_ref[pl.ds(t * pieces, pieces)].reshape(BLOCK, width).astype(F32)

    statistics = [
        join_halves(*(second_ref[c, BLOCKS * BLOCK :, :] for c in range(2)), y)
        for y in range(2)
    ]
    scales = []
    means = []
    for i in range(2):
        y = lax.rem(place_ref[3] + i, 2)

        def load(t):
            block = (t // 2) % 4 * 4 + y * 2 + lax.rem(place_ref[1] + t % 2, 2)
            rows = pl.ds(pl.multiple_of(block * BLOCK, BLOCK), BLOCK)
            return second_ref[t // 8, rows, :].astype(F32)

        center, scale = (jnp.where(y == 0, u, v) for u, v in zip(*statistics))
        sums = jnp.zeros((8, width), F32)
        for t in range(BLOCKS):
            norm = ((load(t) - center) * scale).astype(BF16)
            nb_ref[t * BLOCK : (t + 1) * BLOCK, i * width : (i + 1) * width] = norm
            sums += fold(norm.astype(F32))
        scales.append(scale)
        means.append(sums / count)
    scale_second = jnp.concatenate(scales, axis=1)
    mean_second = jnp.concatenate(means, axis=1)

    center, squares = column_moments(first_block, BLOCKS, count)
    scale_first = lax.rsqrt(jnp.maximum(squares, 0.0) / count + EPSILON)
    sums = jnp.zeros((8, width), F32)
    for t in range(BLOCKS):
        norm = ((first_block(sample_block(place_ref, t)) - center) * scale_first).astype(BF16)
        na_ref[t * BLOCK : (t + 1) * BLOCK, :] = norm
        sums += fold(norm.astype(F32))
    mean_first = sums / count

    correlation = (
        lax.dot_general(
            na_ref[...], nb_ref[...], (((0,), (0,)), ((), ())), preferred_element_type=F32
        )
        / count
    )
    row_ids = lax.broadcasted_iota(jnp.int32, correlation.shape, 0)
    col_ids = lax.broadcasted_iota(jnp.int32, correlation.shape, 1)
    grad = jnp.where(
        row_ids == col_ids + place_ref[2],
        2.0 * (correlation - 1.0),
        2.0 * OFF_WEIGHT * correlation,
    ).astype(BF16)
    grad_wide = grad.astype(F32)
    weighted = grad_wide * correlation
    projection_second = jnp.sum(weighted, axis=0, keepdims=True)
    centering_second = jnp.sum(
        jnp.dot(split_rows(mean_first), grad, preferred_element_type=F32), axis=0, keepdims=True
    )
    for start in range(0, BLOCKS, CHUNK):
        some = slice(start * BLOCK, (start + CHUNK) * BLOCK)
        partial = jnp.dot(na_ref[some, :], grad, preferred_element_type=F32)
        partial = (
            (partial - centering_second - nb_ref[some, :].astype(F32) * projection_second)
            * scale_second
        ).astype(BF16)
        for i in range(2):
            moved_ref[start : start + CHUNK, i] = partial[:, i * width : (i + 1) * width].reshape(
                CHUNK, BLOCK, width
            )

    across = (((1,), (1,)), ((), ()))
    lanes = 128
    folded = sum(weighted[:, i : i + lanes] for i in range(0, 2 * width, lanes))
    projection_first = jnp.sum(folded.T, axis=0, keepdims=True)
    centering_first = jnp.sum(
        lax.dot_general(split_rows(mean_second), grad, across, preferred_element_type=F32),
        axis=0,
        keepdims=True,
    )
    stores = []
    for start in range(0, BLOCKS, CHUNK):
        some = slice(start * BLOCK, (start + CHUNK) * BLOCK)
        partial = lax.dot_general(nb_ref[some, :], grad, across, preferred_element_type=F32)
        partial = (
            partial - centering_first - na_ref[some, :].astype(F32) * projection_first
        ) * scale_first
        out_ref[some, :] = partial.astype(BF16)
        for t in range(start, start + CHUNK):
            row = pl.multiple_of(sample_block(place_ref, t) * BLOCK, BLOCK)
            store = pltpu.make_async_copy(
                out_ref.at[pl.ds(t * BLOCK, BLOCK)],
                out_hbm.at[pl.ds(row, BLOCK)],
                out_sems.at[t],
            )
            store.start()
            stores.append(store)
    for store in stores:
        store.wait()


def spread_kernel(values_ref, out_hbm, halves_ref, sems):
    width = halves_ref.shape[2]
    for i in range(2):
        halves_ref[i] = values_ref[:, i * width : (i + 1) * width]
    copies = [
        pltpu.make_async_copy(halves_ref, out_hbm.at[pl.ds(2 * i, 2)], sems.at[i])
        for i in range(out_hbm.shape[0] // 2)
    ]
    for copy in copies:
        copy.start()
    for copy in copies:
        copy.wait()


def spread_halves(values, copies):
    rows, width = values.shape
    shape = (rows, width // 2)
    return pl.pallas_call(
        spread_kernel,
        out_shape=pltpu.HBM((copies,) + shape, BF16),
        in_specs=[pl.BlockSpec(memory_space=pltpu.VMEM)],
        out_specs=pl.BlockSpec(memory_space=pltpu.HBM),
        scratch_shapes=[pltpu.VMEM((2,) + shape, BF16), pltpu.SemaphoreType.DMA((copies // 2,))],
        cost_estimate=pl.CostEstimate(flops=0, bytes_accessed=2 << 20, transcendentals=0),
    )(values)


def gather_half(parts):
    rows = len(parts) * 4 * BLOCK + 16
    spec = pl.BlockSpec(memory_space=pltpu.VMEM)
    return pl.pallas_call(
        half_kernel,
        out_shape=jax.ShapeDtypeStruct((rows, parts[0].shape[2]), BF16),
        in_specs=[spec] * len(parts),
        out_specs=spec,
        compiler_params=pltpu.CompilerParams(vmem_limit_bytes=VMEM_LIMIT),
        cost_estimate=pl.CostEstimate(flops=4 << 20, bytes_accessed=2 << 20, transcendentals=0),
    )(*parts)


def local_compute(place, first, second):
    count, width = first.shape[0] * first.shape[1], first.shape[2]
    pieces = (BLOCKS, 2, BLOCK, width)
    smem, vmem, hbm = (pl.BlockSpec(memory_space=m) for m in (pltpu.SMEM, pltpu.VMEM, pltpu.HBM))
    return pl.pallas_call(
        tile_kernel,
        out_shape=(jax.ShapeDtypeStruct(pieces, BF16), pltpu.HBM((count, width), BF16)),
        in_specs=[smem, vmem, vmem],
        out_specs=(vmem, hbm),
        scratch_shapes=[
            pltpu.VMEM((count, width), BF16),
            pltpu.VMEM((count, 2 * width), BF16),
            pltpu.VMEM((count, width), BF16),
            pltpu.SemaphoreType.DMA((BLOCKS,)),
        ],
        compiler_params=pltpu.CompilerParams(vmem_limit_bytes=VMEM_LIMIT),
        cost_estimate=pl.CostEstimate(
            flops=12 * count * width * width, bytes_accessed=6 << 20, transcendentals=0
        ),
    )(place, first, second)


def shards(first_view_outputs, second_view_outputs):
    rows_a, width_a = first_view_outputs.shape
    rows_b, width_b = second_view_outputs.shape
    n_dp = lax.axis_size(SAMPLES)
    half = width_a // 2

    near = exchange(jnp.broadcast_to(second_view_outputs, (4, rows_b, width_b)), NEAR)
    spread = spread_halves(first_view_outputs, n_dp)
    near, spread = lax.optimization_barrier((near, spread))

    first = exchange(spread, SAMPLES)

    own = gather_half([near] + [shift(near, -k) for k in (1, 2, 3)])
    own = jnp.broadcast_to(own, (2,) + own.shape)
    first, own = lax.optimization_barrier((first, own))
    second = exchange(own, "core")

    feat = lax.axis_index(FEATURES)
    pair = lax.axis_index(("zh", "yk"))
    place = jnp.stack(
        [
            lax.axis_index("x"),
            lax.axis_index("zl"),
            jnp.where(feat == pair, 0, 2 * width_a),
            lax.axis_index("yl"),
        ]
    ).astype(jnp.int32)
    moved, partial_first = local_compute(place, first, second)

    pieces = exchange(moved.reshape(2, 4, 4, rows_b, width_b), "core")
    pieces = narrow_sum(pieces[0], pieces[1])
    pieces = narrow_sum(pieces[0], *[shift(pieces[k], k) for k in (2, 1, 3)])
    pieces = [pieces[0]] + [near_swap(pieces[k], k) for k in (1, 2, 3)]

    parts = exchange(partial_first.reshape(n_dp, rows_a, half), SAMPLES)
    parts = jnp.sum(parts.reshape(n_dp // 2, 2, rows_a, half).astype(F32), axis=0).astype(BF16)
    first_view_gradient = jnp.concatenate([parts[0], parts[1]], axis=1)
    first_view_gradient, *pieces = lax.optimization_barrier([first_view_gradient] + pieces)
    return first_view_gradient, narrow_sum(*pieces)


def solution(mesh):
    fine = Mesh(
        mesh.devices.reshape(4, 4, 2, 2, 4, 2), ("zh", "yk", "yl", "zl", "x", "core")
    )
    specs = (P(SAMPLES, FEATURES), P(FEATURES, SAMPLES))
    return jax.shard_map(
        shards, mesh=fine, in_specs=specs, out_specs=specs, check_vma=False
    )
```

```python
import functools

import jax
import jax.numpy as jnp
from jax import lax
from jax.experimental import pallas as pl
from jax.experimental.pallas import tpu as pltpu
from jax.sharding import Mesh, PartitionSpec as P

EPSILON = 1e-05
OFF_WEIGHT = 0.0051

SAMPLES = ("zh", "yk", "yl")
FEATURES = ("zl", "x", "core")
NEAR = ("yl", "zl")
F32 = jnp.float32
BF16 = jnp.bfloat16
VMEM_LIMIT = 28 * 1024 * 1024

BLOCK = 128
BLOCKS = 16
CHUNK = 4


def exchange(values, axes):
    return lax.all_to_all(values, axes, 0, 0, tiled=True)


def near_swap(values, move):
    flip = 2 * (move % 2) + move // 2
    return lax.ppermute(values, NEAR, [(i, i ^ flip) for i in range(4)])


def shift(values, distance):
    return lax.ppermute(values, "x", [(i, (i + distance) % 4) for i in range(4)])


def narrow_sum(*terms):
    return sum(term.astype(F32) for term in terms).astype(BF16)


def sample_block(place_ref, t):
    core = t // 8
    x = lax.rem(place_ref[0] + (t // 2) % 4, 4)
    zl = lax.rem(place_ref[1] + t % 2, 2)
    return (zl * 4 + x) * 2 + core


def fold(values):
    return values.reshape(-1, 8, values.shape[-1]).sum(axis=0)


def split_bf16(row):
    rows = []
    for _ in range(3):
        rows.append(row.astype(BF16))
        row = row - rows[-1].astype(F32)
    return rows


def split_rows(sums):
    rows = split_bf16(jnp.sum(sums, axis=0, keepdims=True))
    return jnp.concatenate(rows + [jnp.zeros((13, sums.shape[1]), BF16)], axis=0)


def column_moments(load, blocks, count):
    pivot = jnp.mean(load(0), axis=0, keepdims=True)
    sums = jnp.zeros((8, pivot.shape[1]), F32)
    squares = sums
    for t in range(blocks):
        shifted = load(t) - pivot
        sums += fold(shifted)
        squares += fold(shifted * shifted)
    sums = jnp.sum(sums, axis=0, keepdims=True)
    offset = sums / count
    return pivot + offset, jnp.sum(squares, axis=0, keepdims=True) - offset * sums


def half_kernel(*refs):
    block_refs, out_ref = refs[:-1], refs[-1]
    blocks = len(block_refs) * 2
    rows = []
    for y in range(2):
        load = lambda t: block_refs[t // 2][2 * y + t % 2].astype(F32)
        mean, squares = column_moments(load, blocks, blocks * BLOCK)
        rows += split_bf16(mean) + split_bf16(squares)
    rows.append(jnp.zeros((4, rows[0].shape[1]), BF16))
    for x, ref in enumerate(block_refs):
        for i in range(4):
            row = (x * 4 + i) * BLOCK
            out_ref[row : row + BLOCK, :] = ref[i]
    out_ref[len(block_refs) * 4 * BLOCK :, :] = jnp.concatenate(rows, axis=0)


def join_halves(first, second, y):
    first, second = first.astype(F32), second.astype(F32)

    def value(rows, i):
        return sum(rows[y * 6 + i * 3 + k : y * 6 + i * 3 + k + 1] for k in range(3))

    count = BLOCKS * BLOCK
    apart = value(first, 0) - value(second, 0)
    squares = value(first, 1) + value(second, 1) + apart * apart * (count / 4)
    mean = 0.5 * (value(first, 0) + value(second, 0))
    return mean, lax.rsqrt(jnp.maximum(squares, 0.0) / count + EPSILON)


def tile_kernel(
    place_ref, first_ref, second_ref, moved_ref, out_hbm,
    na_ref, nb_ref, out_ref, out_sems,
):
    count = BLOCK * BLOCKS
    width = first_ref.shape[2]
    pieces = BLOCK // first_ref.shape[1]

    def first_block(t):
        return first_ref[pl.ds(t * pieces, pieces)].reshape(BLOCK, width).astype(F32)

    statistics = [
        join_halves(*(second_ref[c, BLOCKS * BLOCK :, :] for c in range(2)), y)
        for y in range(2)
    ]
    scales = []
    means = []
    for i in range(2):
        y = lax.rem(place_ref[3] + i, 2)

        def load(t):
            block = (t // 2) % 4 * 4 + y * 2 + lax.rem(place_ref[1] + t % 2, 2)
            rows = pl.ds(pl.multiple_of(block * BLOCK, BLOCK), BLOCK)
            return second_ref[t // 8, rows, :].astype(F32)

        center, scale = (jnp.where(y == 0, u, v) for u, v in zip(*statistics))
        sums = jnp.zeros((8, width), F32)
        for t in range(BLOCKS):
            norm = ((load(t) - center) * scale).astype(BF16)
            nb_ref[t * BLOCK : (t + 1) * BLOCK, i * width : (i + 1) * width] = norm
            sums += fold(norm.astype(F32))
        scales.append(scale)
        means.append(sums / count)
    scale_second = jnp.concatenate(scales, axis=1)
    mean_second = jnp.concatenate(means, axis=1)

    center, squares = column_moments(first_block, BLOCKS, count)
    scale_first = lax.rsqrt(jnp.maximum(squares, 0.0) / count + EPSILON)
    sums = jnp.zeros((8, width), F32)
    for t in range(BLOCKS):
        norm = ((first_block(sample_block(place_ref, t)) - center) * scale_first).astype(BF16)
        na_ref[t * BLOCK : (t + 1) * BLOCK, :] = norm
        sums += fold(norm.astype(F32))
    mean_first = sums / count

    correlation = (
        lax.dot_general(
            na_ref[...], nb_ref[...], (((0,), (0,)), ((), ())), preferred_element_type=F32
        )
        / count
    )
    row_ids = lax.broadcasted_iota(jnp.int32, correlation.shape, 0)
    col_ids = lax.broadcasted_iota(jnp.int32, correlation.shape, 1)
    grad = jnp.where(
        row_ids == col_ids + place_ref[2],
        2.0 * (correlation - 1.0),
        2.0 * OFF_WEIGHT * correlation,
    ).astype(BF16)
    grad_wide = grad.astype(F32)
    weighted = grad_wide * correlation
    projection_second = jnp.sum(weighted, axis=0, keepdims=True)
    centering_second = jnp.sum(
        jnp.dot(split_rows(mean_first), grad, preferred_element_type=F32), axis=0, keepdims=True
    )
    for start in range(0, BLOCKS, CHUNK):
        some = slice(start * BLOCK, (start + CHUNK) * BLOCK)
        partial = jnp.dot(na_ref[some, :], grad, preferred_element_type=F32)
        partial = (
            (partial - centering_second - nb_ref[some, :].astype(F32) * projection_second)
            * scale_second
        ).astype(BF16)
        for i in range(2):
            moved_ref[start : start + CHUNK, i] = partial[:, i * width : (i + 1) * width].reshape(
                CHUNK, BLOCK, width
            )

    across = (((1,), (1,)), ((), ()))
    lanes = 128
    folded = sum(weighted[:, i : i + lanes] for i in range(0, 2 * width, lanes))
    projection_first = jnp.sum(folded.T, axis=0, keepdims=True)
    centering_first = jnp.sum(
        lax.dot_general(split_rows(mean_second), grad, across, preferred_element_type=F32),
        axis=0,
        keepdims=True,
    )
    stores = []
    for start in range(0, BLOCKS, CHUNK):
        some = slice(start * BLOCK, (start + CHUNK) * BLOCK)
        partial = lax.dot_general(nb_ref[some, :], grad, across, preferred_element_type=F32)
        partial = (
            partial - centering_first - na_ref[some, :].astype(F32) * projection_first
        ) * scale_first
        out_ref[some, :] = partial.astype(BF16)
        for t in range(start, start + CHUNK):
            row = pl.multiple_of(sample_block(place_ref, t) * BLOCK, BLOCK)
            store = pltpu.make_async_copy(
                out_ref.at[pl.ds(t * BLOCK, BLOCK)],
                out_hbm.at[pl.ds(row, BLOCK)],
                out_sems.at[t],
            )
            store.start()
            stores.append(store)
    for store in stores:
        store.wait()


def spread_kernel(values_ref, out_hbm, halves_ref, sems):
    width = halves_ref.shape[2]
    for i in range(2):
        halves_ref[i] = values_ref[:, i * width : (i + 1) * width]
    copies = [
        pltpu.make_async_copy(halves_ref, out_hbm.at[pl.ds(2 * i, 2)], sems.at[i])
        for i in range(out_hbm.shape[0] // 2)
    ]
    for copy in copies:
        copy.start()
    for copy in copies:
        copy.wait()


def spread_halves(values, copies):
    rows, width = values.shape
    shape = (rows, width // 2)
    return pl.pallas_call(
        spread_kernel,
        out_shape=pltpu.HBM((copies,) + shape, BF16),
        in_specs=[pl.BlockSpec(memory_space=pltpu.VMEM)],
        out_specs=pl.BlockSpec(memory_space=pltpu.HBM),
        scratch_shapes=[pltpu.VMEM((2,) + shape, BF16), pltpu.SemaphoreType.DMA((copies // 2,))],
        cost_estimate=pl.CostEstimate(flops=0, bytes_accessed=2 << 20, transcendentals=0),
    )(values)


def gather_half(parts):
    rows = len(parts) * 4 * BLOCK + 16
    spec = pl.BlockSpec(memory_space=pltpu.VMEM)
    return pl.pallas_call(
        half_kernel,
        out_shape=jax.ShapeDtypeStruct((rows, parts[0].shape[2]), BF16),
        in_specs=[spec] * len(parts),
        out_specs=spec,
        compiler_params=pltpu.CompilerParams(vmem_limit_bytes=VMEM_LIMIT),
        cost_estimate=pl.CostEstimate(flops=4 << 20, bytes_accessed=2 << 20, transcendentals=0),
    )(*parts)


def local_compute(place, first, second):
    count, width = first.shape[0] * first.shape[1], first.shape[2]
    pieces = (BLOCKS, 2, BLOCK, width)
    smem, vmem, hbm = (pl.BlockSpec(memory_space=m) for m in (pltpu.SMEM, pltpu.VMEM, pltpu.HBM))
    return pl.pallas_call(
        tile_kernel,
        out_shape=(jax.ShapeDtypeStruct(pieces, BF16), pltpu.HBM((count, width), BF16)),
        in_specs=[smem, vmem, vmem],
        out_specs=(vmem, hbm),
        scratch_shapes=[
            pltpu.VMEM((count, width), BF16),
            pltpu.VMEM((count, 2 * width), BF16),
            pltpu.VMEM((count, width), BF16),
            pltpu.SemaphoreType.DMA((BLOCKS,)),
        ],
        compiler_params=pltpu.CompilerParams(vmem_limit_bytes=VMEM_LIMIT),
        cost_estimate=pl.CostEstimate(
            flops=12 * count * width * width, bytes_accessed=6 << 20, transcendentals=0
        ),
    )(place, first, second)


def shards(first_view_outputs, second_view_outputs):
    rows_a, width_a = first_view_outputs.shape
    rows_b, width_b = second_view_outputs.shape
    n_dp = lax.axis_size(SAMPLES)
    half = width_a // 2

    spread = spread_halves(first_view_outputs, n_dp)
    spread, local = lax.optimization_barrier((spread, second_view_outputs))
    near = exchange(jnp.broadcast_to(local, (4, rows_b, width_b)), NEAR)
    near, spread = lax.optimization_barrier((near, spread))

    first = exchange(spread, SAMPLES)

    own = gather_half([near] + [shift(near, -k) for k in (1, 2, 3)])
    own = jnp.broadcast_to(own, (2,) + own.shape)
    first, own = lax.optimization_barrier((first, own))
    second = exchange(own, "core")

    feat = lax.axis_index(FEATURES)
    pair = lax.axis_index(("zh", "yk"))
    place = jnp.stack(
        [
            lax.axis_index("x"),
            lax.axis_index("zl"),
            jnp.where(feat == pair, 0, 2 * width_a),
            lax.axis_index("yl"),
        ]
    ).astype(jnp.int32)
    moved, partial_first = local_compute(place, first, second)

    pieces = exchange(moved.reshape(2, 4, 4, rows_b, width_b), "core")
    pieces = narrow_sum(pieces[0], pieces[1])
    pieces = narrow_sum(pieces[0], *[shift(pieces[k], k) for k in (2, 1, 3)])
    pieces = [pieces[0]] + [near_swap(pieces[k], k) for k in (1, 2, 3)]

    parts = exchange(partial_first.reshape(n_dp, rows_a, half), SAMPLES)
    parts = jnp.sum(parts.reshape(n_dp // 2, 2, rows_a, half).astype(F32), axis=0).astype(BF16)
    first_view_gradient = jnp.concatenate([parts[0], parts[1]], axis=1)
    first_view_gradient, *pieces = lax.optimization_barrier([first_view_gradient] + pieces)
    return first_view_gradient, narrow_sum(*pieces)


def solution(mesh):
    fine = Mesh(
        mesh.devices.reshape(4, 4, 2, 2, 4, 2), ("zh", "yk", "yl", "zl", "x", "core")
    )
    specs = (P(SAMPLES, FEATURES), P(FEATURES, SAMPLES))
    return jax.shard_map(
        shards, mesh=fine, in_specs=specs, out_specs=specs, check_vma=False
    )
```

```python
import functools

import jax
import jax.numpy as jnp
from jax import lax
from jax.experimental import pallas as pl
from jax.experimental.pallas import tpu as pltpu
from jax.sharding import Mesh, PartitionSpec as P

EPSILON = 1e-05
OFF_WEIGHT = 0.0051

SAMPLES = ("zh", "yk", "yl")
FEATURES = ("zl", "x", "core")
NEAR = ("yl", "zl")
F32 = jnp.float32
BF16 = jnp.bfloat16
VMEM_LIMIT = 28 * 1024 * 1024

BLOCK = 128
BLOCKS = 16
CHUNK = 2


def exchange(values, axes):
    return lax.all_to_all(values, axes, 0, 0, tiled=True)


def near_swap(values, move):
    flip = 2 * (move % 2) + move // 2
    return lax.ppermute(values, NEAR, [(i, i ^ flip) for i in range(4)])


def shift(values, distance):
    return lax.ppermute(values, "x", [(i, (i + distance) % 4) for i in range(4)])


def narrow_sum(*terms):
    return sum(term.astype(F32) for term in terms).astype(BF16)


def sample_block(place_ref, t):
    core = t // 8
    x = lax.rem(place_ref[0] + (t // 2) % 4, 4)
    zl = lax.rem(place_ref[1] + t % 2, 2)
    return (zl * 4 + x) * 2 + core


def fold(values):
    return values.reshape(-1, 8, values.shape[-1]).sum(axis=0)


def split_bf16(row):
    rows = []
    for _ in range(3):
        rows.append(row.astype(BF16))
        row = row - rows[-1].astype(F32)
    return rows


def split_rows(sums):
    rows = split_bf16(jnp.sum(sums, axis=0, keepdims=True))
    return jnp.concatenate(rows + [jnp.zeros((13, sums.shape[1]), BF16)], axis=0)


def column_moments(load, blocks, count):
    pivot = jnp.mean(load(0), axis=0, keepdims=True)
    sums = jnp.zeros((8, pivot.shape[1]), F32)
    squares = sums
    for t in range(blocks):
        shifted = load(t) - pivot
        sums += fold(shifted)
        squares += fold(shifted * shifted)
    sums = jnp.sum(sums, axis=0, keepdims=True)
    offset = sums / count
    return pivot + offset, jnp.sum(squares, axis=0, keepdims=True) - offset * sums


def half_kernel(*refs):
    block_refs, out_ref = refs[:-1], refs[-1]
    blocks = len(block_refs) * 2
    rows = []
    for y in range(2):
        load = lambda t: block_refs[t // 2][2 * y + t % 2].astype(F32)
        mean, squares = column_moments(load, blocks, blocks * BLOCK)
        rows += split_bf16(mean) + split_bf16(squares)
    rows.append(jnp.zeros((4, rows[0].shape[1]), BF16))
    for x, ref in enumerate(block_refs):
        for i in range(4):
            row = (x * 4 + i) * BLOCK
            out_ref[row : row + BLOCK, :] = ref[i]
    out_ref[len(block_refs) * 4 * BLOCK :, :] = jnp.concatenate(rows, axis=0)


def join_halves(first, second, y):
    first, second = first.astype(F32), second.astype(F32)

    def value(rows, i):
        return sum(rows[y * 6 + i * 3 + k : y * 6 + i * 3 + k + 1] for k in range(3))

    count = BLOCKS * BLOCK
    apart = value(first, 0) - value(second, 0)
    squares = value(first, 1) + value(second, 1) + apart * apart * (count / 4)
    mean = 0.5 * (value(first, 0) + value(second, 0))
    return mean, lax.rsqrt(jnp.maximum(squares, 0.0) / count + EPSILON)


def tile_kernel(
    place_ref, first_ref, second_ref, moved_ref, out_hbm,
    na_ref, nb_ref, out_ref, out_sems,
):
    count = BLOCK * BLOCKS
    width = first_ref.shape[2]
    pieces = BLOCK // first_ref.shape[1]

    def first_block(t):
        return first_ref[pl.ds(t * pieces, pieces)].reshape(BLOCK, width).astype(F32)

    statistics = [
        join_halves(*(second_ref[c, BLOCKS * BLOCK :, :] for c in range(2)), y)
        for y in range(2)
    ]
    scales = []
    means = []
    for i in range(2):
        y = lax.rem(place_ref[3] + i, 2)

        def load(t):
            block = (t // 2) % 4 * 4 + y * 2 + lax.rem(place_ref[1] + t % 2, 2)
            rows = pl.ds(pl.multiple_of(block * BLOCK, BLOCK), BLOCK)
            return second_ref[t // 8, rows, :].astype(F32)

        center, scale = (jnp.where(y == 0, u, v) for u, v in zip(*statistics))
        sums = jnp.zeros((8, width), F32)
        for t in range(BLOCKS):
            norm = ((load(t) - center) * scale).astype(BF16)
            nb_ref[t * BLOCK : (t + 1) * BLOCK, i * width : (i + 1) * width] = norm
            sums += fold(norm.astype(F32))
        scales.append(scale)
        means.append(sums / count)
    scale_second = jnp.concatenate(scales, axis=1)
    mean_second = jnp.concatenate(means, axis=1)

    center, squares = column_moments(first_block, BLOCKS, count)
    scale_first = lax.rsqrt(jnp.maximum(squares, 0.0) / count + EPSILON)
    sums = jnp.zeros((8, width), F32)
    for t in range(BLOCKS):
        norm = ((first_block(sample_block(place_ref, t)) - center) * scale_first).astype(BF16)
        na_ref[t * BLOCK : (t + 1) * BLOCK, :] = norm
        sums += fold(norm.astype(F32))
    mean_first = sums / count

    correlation = (
        lax.dot_general(
            na_ref[...], nb_ref[...], (((0,), (0,)), ((), ())), preferred_element_type=F32
        )
        / count
    )
    row_ids = lax.broadcasted_iota(jnp.int32, correlation.shape, 0)
    col_ids = lax.broadcasted_iota(jnp.int32, correlation.shape, 1)
    grad = jnp.where(
        row_ids == col_ids + place_ref[2],
        2.0 * (correlation - 1.0),
        2.0 * OFF_WEIGHT * correlation,
    ).astype(BF16)
    grad_wide = grad.astype(F32)
    weighted = grad_wide * correlation
    projection_second = jnp.sum(weighted, axis=0, keepdims=True)
    centering_second = jnp.sum(
        jnp.dot(split_rows(mean_first), grad, preferred_element_type=F32), axis=0, keepdims=True
    )
    grad_second = (grad_wide * scale_second).astype(BF16)
    centering_second *= scale_second
    projection_second *= scale_second
    for start in range(0, BLOCKS, CHUNK):
        some = slice(start * BLOCK, (start + CHUNK) * BLOCK)
        partial = jnp.dot(na_ref[some, :], grad_second, preferred_element_type=F32)
        partial = (
            partial - centering_second - nb_ref[some, :].astype(F32) * projection_second
        ).astype(BF16)
        for i in range(2):
            moved_ref[start : start + CHUNK, i] = partial[:, i * width : (i + 1) * width].reshape(
                CHUNK, BLOCK, width
            )

    across = (((1,), (1,)), ((), ()))
    lanes = 128
    folded = sum(weighted[:, i : i + lanes] for i in range(0, 2 * width, lanes))
    projection_first = jnp.sum(folded.T, axis=0, keepdims=True)
    centering_first = jnp.sum(
        lax.dot_general(split_rows(mean_second), grad, across, preferred_element_type=F32),
        axis=0,
        keepdims=True,
    )
    scale_rows = jnp.broadcast_to(scale_first, (lanes, width)).T[:, :1]
    grad_first = (grad_wide * scale_rows).astype(BF16)
    centering_first *= scale_first
    projection_first *= scale_first
    stores = []
    for start in range(0, BLOCKS, CHUNK):
        some = slice(start * BLOCK, (start + CHUNK) * BLOCK)
        partial = lax.dot_general(nb_ref[some, :], grad_first, across, preferred_element_type=F32)
        partial = partial - centering_first - na_ref[some, :].astype(F32) * projection_first
        out_ref[some, :] = partial.astype(BF16)
        for t in range(start, start + CHUNK):
            row = pl.multiple_of(sample_block(place_ref, t) * BLOCK, BLOCK)
            store = pltpu.make_async_copy(
                out_ref.at[pl.ds(t * BLOCK, BLOCK)],
                out_hbm.at[pl.ds(row, BLOCK)],
                out_sems.at[t],
            )
            store.start()
            stores.append(store)
    for store in stores:
        store.wait()


def spread_kernel(values_ref, out_hbm, halves_ref, sems):
    width = halves_ref.shape[2]
    for i in range(2):
        halves_ref[i] = values_ref[:, i * width : (i + 1) * width]
    copies = [
        pltpu.make_async_copy(halves_ref, out_hbm.at[pl.ds(2 * i, 2)], sems.at[i])
        for i in range(out_hbm.shape[0] // 2)
    ]
    for copy in copies:
        copy.start()
    for copy in copies:
        copy.wait()


def spread_halves(values, copies):
    rows, width = values.shape
    shape = (rows, width // 2)
    return pl.pallas_call(
        spread_kernel,
        out_shape=pltpu.HBM((copies,) + shape, BF16),
        in_specs=[pl.BlockSpec(memory_space=pltpu.VMEM)],
        out_specs=pl.BlockSpec(memory_space=pltpu.HBM),
        scratch_shapes=[pltpu.VMEM((2,) + shape, BF16), pltpu.SemaphoreType.DMA((copies // 2,))],
        cost_estimate=pl.CostEstimate(flops=0, bytes_accessed=2 << 20, transcendentals=0),
    )(values)


def gather_half(parts):
    rows = len(parts) * 4 * BLOCK + 16
    spec = pl.BlockSpec(memory_space=pltpu.VMEM)
    return pl.pallas_call(
        half_kernel,
        out_shape=jax.ShapeDtypeStruct((rows, parts[0].shape[2]), BF16),
        in_specs=[spec] * len(parts),
        out_specs=spec,
        compiler_params=pltpu.CompilerParams(vmem_limit_bytes=VMEM_LIMIT),
        cost_estimate=pl.CostEstimate(flops=4 << 20, bytes_accessed=2 << 20, transcendentals=0),
    )(*parts)


def local_compute(place, first, second):
    count, width = first.shape[0] * first.shape[1], first.shape[2]
    pieces = (BLOCKS, 2, BLOCK, width)
    smem, vmem, hbm = (pl.BlockSpec(memory_space=m) for m in (pltpu.SMEM, pltpu.VMEM, pltpu.HBM))
    return pl.pallas_call(
        tile_kernel,
        out_shape=(jax.ShapeDtypeStruct(pieces, BF16), pltpu.HBM((count, width), BF16)),
        in_specs=[smem, vmem, vmem],
        out_specs=(vmem, hbm),
        scratch_shapes=[
            pltpu.VMEM((count, width), BF16),
            pltpu.VMEM((count, 2 * width), BF16),
            pltpu.VMEM((count, width), BF16),
            pltpu.SemaphoreType.DMA((BLOCKS,)),
        ],
        compiler_params=pltpu.CompilerParams(vmem_limit_bytes=VMEM_LIMIT),
        cost_estimate=pl.CostEstimate(
            flops=12 * count * width * width, bytes_accessed=6 << 20, transcendentals=0
        ),
    )(place, first, second)


def shards(first_view_outputs, second_view_outputs):
    rows_a, width_a = first_view_outputs.shape
    rows_b, width_b = second_view_outputs.shape
    n_dp = lax.axis_size(SAMPLES)
    half = width_a // 2

    near = exchange(jnp.broadcast_to(second_view_outputs, (4, rows_b, width_b)), NEAR)
    spread = spread_halves(first_view_outputs, n_dp)
    near, spread = lax.optimization_barrier((near, spread))

    first = exchange(spread, SAMPLES)

    own = gather_half([near] + [shift(near, -k) for k in (1, 2, 3)])
    own = jnp.broadcast_to(own, (2,) + own.shape)
    first, own = lax.optimization_barrier((first, own))
    second = exchange(own, "core")

    feat = lax.axis_index(FEATURES)
    pair = lax.axis_index(("zh", "yk"))
    place = jnp.stack(
        [
            lax.axis_index("x"),
            lax.axis_index("zl"),
            jnp.where(feat == pair, 0, 2 * width_a),
            lax.axis_index("yl"),
        ]
    ).astype(jnp.int32)
    moved, partial_first = local_compute(place, first, second)

    pieces = exchange(moved.reshape(2, 4, 4, rows_b, width_b), "core")
    pieces = narrow_sum(pieces[0], pieces[1])
    pieces = narrow_sum(pieces[0], *[shift(pieces[k], k) for k in (2, 1, 3)])
    pieces = [pieces[0]] + [near_swap(pieces[k], k) for k in (1, 2, 3)]

    parts = exchange(partial_first.reshape(n_dp, rows_a, half), SAMPLES)
    parts = jnp.sum(parts.reshape(n_dp // 2, 2, rows_a, half).astype(F32), axis=0).astype(BF16)
    first_view_gradient = jnp.concatenate([parts[0], parts[1]], axis=1)
    first_view_gradient, *pieces = lax.optimization_barrier([first_view_gradient] + pieces)
    return first_view_gradient, narrow_sum(*pieces)


def solution(mesh):
    fine = Mesh(
        mesh.devices.reshape(4, 4, 2, 2, 4, 2), ("zh", "yk", "yl", "zl", "x", "core")
    )
    specs = (P(SAMPLES, FEATURES), P(FEATURES, SAMPLES))
    return jax.shard_map(
        shards, mesh=fine, in_specs=specs, out_specs=specs, check_vma=False
    )
```

```python
import functools

import jax
import jax.numpy as jnp
from jax import lax
from jax.experimental import pallas as pl
from jax.experimental.pallas import tpu as pltpu
from jax.sharding import Mesh, PartitionSpec as P

EPSILON = 1e-05
OFF_WEIGHT = 0.0051

SAMPLES = ("zh", "yk", "yl")
FEATURES = ("zl", "x", "core")
NEAR = ("yl", "zl")
F32 = jnp.float32
BF16 = jnp.bfloat16
VMEM_LIMIT = 28 * 1024 * 1024

BLOCK = 128
BLOCKS = 16
CHUNK = 2


def exchange(values, axes):
    return lax.all_to_all(values, axes, 0, 0, tiled=True)


def near_swap(values, move):
    flip = 2 * (move % 2) + move // 2
    return lax.ppermute(values, NEAR, [(i, i ^ flip) for i in range(4)])


def shift(values, distance):
    return lax.ppermute(values, "x", [(i, (i + distance) % 4) for i in range(4)])


def narrow_sum(*terms):
    return sum(term.astype(F32) for term in terms).astype(BF16)


def sample_block(place_ref, t):
    core = t // 8
    x = lax.rem(place_ref[0] + (t // 2) % 4, 4)
    zl = lax.rem(place_ref[1] + t % 2, 2)
    return (zl * 4 + x) * 2 + core


def fold(values):
    return values.reshape(-1, 8, values.shape[-1]).sum(axis=0)


def split_bf16(row):
    rows = []
    for _ in range(3):
        rows.append(row.astype(BF16))
        row = row - rows[-1].astype(F32)
    return rows


def split_rows(sums):
    rows = split_bf16(jnp.sum(sums, axis=0, keepdims=True))
    return jnp.concatenate(rows + [jnp.zeros((13, sums.shape[1]), BF16)], axis=0)


def column_moments(load, blocks, count):
    pivot = jnp.mean(load(0), axis=0, keepdims=True)
    sums = jnp.zeros((8, pivot.shape[1]), F32)
    squares = sums
    for t in range(blocks):
        shifted = load(t) - pivot
        sums += fold(shifted)
        squares += fold(shifted * shifted)
    sums = jnp.sum(sums, axis=0, keepdims=True)
    offset = sums / count
    return pivot + offset, jnp.sum(squares, axis=0, keepdims=True) - offset * sums


def half_kernel(*refs):
    block_refs, out_ref = refs[:-1], refs[-1]
    blocks = len(block_refs) * 2
    rows = []
    for y in range(2):
        load = lambda t: block_refs[t // 2][2 * y + t % 2].astype(F32)
        mean, squares = column_moments(load, blocks, blocks * BLOCK)
        rows += split_bf16(mean) + split_bf16(squares)
    rows.append(jnp.zeros((4, rows[0].shape[1]), BF16))
    for x, ref in enumerate(block_refs):
        for i in range(4):
            row = (x * 4 + i) * BLOCK
            out_ref[row : row + BLOCK, :] = ref[i]
    out_ref[len(block_refs) * 4 * BLOCK :, :] = jnp.concatenate(rows, axis=0)


def join_halves(first, second, y):
    first, second = first.astype(F32), second.astype(F32)

    def value(rows, i):
        return sum(rows[y * 6 + i * 3 + k : y * 6 + i * 3 + k + 1] for k in range(3))

    count = BLOCKS * BLOCK
    apart = value(first, 0) - value(second, 0)
    squares = value(first, 1) + value(second, 1) + apart * apart * (count / 4)
    mean = 0.5 * (value(first, 0) + value(second, 0))
    return mean, lax.rsqrt(jnp.maximum(squares, 0.0) / count + EPSILON)


def tile_kernel(
    place_ref, first_ref, second_ref, moved_ref, out_hbm,
    na_ref, nb_ref, out_ref, out_sems,
):
    count = BLOCK * BLOCKS
    width = first_ref.shape[2]
    pieces = BLOCK // first_ref.shape[1]

    def first_block(t):
        return first_ref[pl.ds(t * pieces, pieces)].reshape(BLOCK, width).astype(F32)

    statistics = [
        join_halves(*(second_ref[c, BLOCKS * BLOCK :, :] for c in range(2)), y)
        for y in range(2)
    ]
    scales = []
    means = []
    for i in range(2):
        y = lax.rem(place_ref[3] + i, 2)

        def load(t):
            block = (t // 2) % 4 * 4 + y * 2 + lax.rem(place_ref[1] + t % 2, 2)
            rows = pl.ds(pl.multiple_of(block * BLOCK, BLOCK), BLOCK)
            return second_ref[t // 8, rows, :].astype(F32)

        center, scale = (jnp.where(y == 0, u, v) for u, v in zip(*statistics))
        sums = jnp.zeros((8, width), F32)
        for t in range(BLOCKS):
            norm = ((load(t) - center) * scale).astype(BF16)
            nb_ref[t * BLOCK : (t + 1) * BLOCK, i * width : (i + 1) * width] = norm
            sums += fold(norm.astype(F32))
        scales.append(scale)
        means.append(sums / count)
    scale_second = jnp.concatenate(scales, axis=1)
    mean_second = jnp.concatenate(means, axis=1)

    center, squares = column_moments(first_block, BLOCKS, count)
    scale_first = lax.rsqrt(jnp.maximum(squares, 0.0) / count + EPSILON)
    sums = jnp.zeros((8, width), F32)
    for t in range(BLOCKS):
        norm = ((first_block(sample_block(place_ref, t)) - center) * scale_first).astype(BF16)
        na_ref[t * BLOCK : (t + 1) * BLOCK, :] = norm
        sums += fold(norm.astype(F32))
    mean_first = sums / count

    correlation = (
        lax.dot_general(
            na_ref[...], nb_ref[...], (((0,), (0,)), ((), ())), preferred_element_type=F32
        )
        / count
    )
    row_ids = lax.broadcasted_iota(jnp.int32, correlation.shape, 0)
    col_ids = lax.broadcasted_iota(jnp.int32, correlation.shape, 1)
    grad = jnp.where(
        row_ids == col_ids + place_ref[2],
        2.0 * (correlation - 1.0),
        2.0 * OFF_WEIGHT * correlation,
    ).astype(BF16)
    grad_wide = grad.astype(F32)
    weighted = grad_wide * correlation
    projection_second = jnp.sum(weighted, axis=0, keepdims=True)
    centering_second = jnp.sum(
        jnp.dot(split_rows(mean_first), grad, preferred_element_type=F32), axis=0, keepdims=True
    )
    grad_second = (grad_wide * scale_second).astype(BF16)
    centering_second *= scale_second
    projection_second *= scale_second
    for start in range(0, BLOCKS, CHUNK):
        some = slice(start * BLOCK, (start + CHUNK) * BLOCK)
        partial = jnp.dot(na_ref[some, :], grad_second, preferred_element_type=F32)
        partial = (
            partial - centering_second - nb_ref[some, :].astype(F32) * projection_second
        ).astype(BF16)
        for i in range(2):
            moved_ref[start : start + CHUNK, i] = partial[:, i * width : (i + 1) * width].reshape(
                CHUNK, BLOCK, width
            )

    across = (((1,), (1,)), ((), ()))
    lanes = 128
    folded = sum(weighted[:, i : i + lanes] for i in range(0, 2 * width, lanes))
    projection_first = jnp.sum(folded.T, axis=0, keepdims=True)
    centering_first = jnp.sum(
        lax.dot_general(split_rows(mean_second), grad, across, preferred_element_type=F32),
        axis=0,
        keepdims=True,
    )
    scale_rows = jnp.broadcast_to(scale_first, (lanes, width)).T[:, :1]
    grad_first = (grad_wide * scale_rows).astype(BF16)
    centering_first *= scale_first
    projection_first *= scale_first
    stores = []
    for start in range(0, BLOCKS, CHUNK):
        some = slice(start * BLOCK, (start + CHUNK) * BLOCK)
        partial = lax.dot_general(nb_ref[some, :], grad_first, across, preferred_element_type=F32)
        partial = partial - centering_first - na_ref[some, :].astype(F32) * projection_first
        out_ref[some, :] = partial.astype(BF16)
        for t in range(start, start + CHUNK):
            row = pl.multiple_of(sample_block(place_ref, t) * BLOCK, BLOCK)
            store = pltpu.make_async_copy(
                out_ref.at[pl.ds(t * BLOCK, BLOCK)],
                out_hbm.at[pl.ds(row, BLOCK)],
                out_sems.at[t],
            )
            store.start()
            stores.append(store)
    for store in stores:
        store.wait()


def spread_kernel(values_ref, out_hbm, halves_ref, sems):
    width = halves_ref.shape[2]
    for i in range(2):
        halves_ref[i] = values_ref[:, i * width : (i + 1) * width]
    copies = [
        pltpu.make_async_copy(halves_ref, out_hbm.at[pl.ds(2 * i, 2)], sems.at[i])
        for i in range(out_hbm.shape[0] // 2)
    ]
    for copy in copies:
        copy.start()
    for copy in copies:
        copy.wait()


def spread_halves(values, copies):
    rows, width = values.shape
    shape = (rows, width // 2)
    return pl.pallas_call(
        spread_kernel,
        out_shape=pltpu.HBM((copies,) + shape, BF16),
        in_specs=[pl.BlockSpec(memory_space=pltpu.VMEM)],
        out_specs=pl.BlockSpec(memory_space=pltpu.HBM),
        scratch_shapes=[pltpu.VMEM((2,) + shape, BF16), pltpu.SemaphoreType.DMA((copies // 2,))],
        cost_estimate=pl.CostEstimate(flops=0, bytes_accessed=2 << 20, transcendentals=0),
    )(values)


def repeat_kernel(values_hbm, out_hbm, sems):
    copies = [
        pltpu.make_async_copy(values_hbm, out_hbm.at[i], sems.at[i]) for i in range(out_hbm.shape[0])
    ]
    for copy in copies:
        copy.start()
    for copy in copies:
        copy.wait()


def repeat(values, copies):
    hbm = pl.BlockSpec(memory_space=pltpu.HBM)
    return pl.pallas_call(
        repeat_kernel,
        out_shape=pltpu.HBM((copies,) + values.shape, BF16),
        in_specs=[hbm],
        out_specs=hbm,
        scratch_shapes=[pltpu.SemaphoreType.DMA((copies,))],
    )(values)


def gather_half(parts):
    rows = len(parts) * 4 * BLOCK + 16
    spec = pl.BlockSpec(memory_space=pltpu.VMEM)
    return pl.pallas_call(
        half_kernel,
        out_shape=jax.ShapeDtypeStruct((rows, parts[0].shape[2]), BF16),
        in_specs=[spec] * len(parts),
        out_specs=spec,
        compiler_params=pltpu.CompilerParams(vmem_limit_bytes=VMEM_LIMIT),
        cost_estimate=pl.CostEstimate(flops=4 << 20, bytes_accessed=2 << 20, transcendentals=0),
    )(*parts)


def local_compute(place, first, second):
    count, width = first.shape[0] * first.shape[1], first.shape[2]
    pieces = (BLOCKS, 2, BLOCK, width)
    smem, vmem, hbm = (pl.BlockSpec(memory_space=m) for m in (pltpu.SMEM, pltpu.VMEM, pltpu.HBM))
    return pl.pallas_call(
        tile_kernel,
        out_shape=(jax.ShapeDtypeStruct(pieces, BF16), pltpu.HBM((count, width), BF16)),
        in_specs=[smem, vmem, vmem],
        out_specs=(vmem, hbm),
        scratch_shapes=[
            pltpu.VMEM((count, width), BF16),
            pltpu.VMEM((count, 2 * width), BF16),
            pltpu.VMEM((count, width), BF16),
            pltpu.SemaphoreType.DMA((BLOCKS,)),
        ],
        compiler_params=pltpu.CompilerParams(vmem_limit_bytes=VMEM_LIMIT),
        cost_estimate=pl.CostEstimate(
            flops=12 * count * width * width, bytes_accessed=6 << 20, transcendentals=0
        ),
    )(place, first, second)


def shards(first_view_outputs, second_view_outputs):
    rows_a, width_a = first_view_outputs.shape
    rows_b, width_b = second_view_outputs.shape
    n_dp = lax.axis_size(SAMPLES)
    half = width_a // 2

    near = exchange(repeat(second_view_outputs, 4), NEAR)
    spread = spread_halves(first_view_outputs, n_dp)
    near, spread = lax.optimization_barrier((near, spread))

    first = exchange(spread, SAMPLES)

    own = gather_half([near] + [shift(near, -k) for k in (1, 2, 3)])
    own = jnp.broadcast_to(own, (2,) + own.shape)
    first, own = lax.optimization_barrier((first, own))
    second = exchange(own, "core")

    feat = lax.axis_index(FEATURES)
    pair = lax.axis_index(("zh", "yk"))
    place = jnp.stack(
        [
            lax.axis_index("x"),
            lax.axis_index("zl"),
            jnp.where(feat == pair, 0, 2 * width_a),
            lax.axis_index("yl"),
        ]
    ).astype(jnp.int32)
    moved, partial_first = local_compute(place, first, second)

    pieces = exchange(moved.reshape(2, 4, 4, rows_b, width_b), "core")
    pieces = narrow_sum(pieces[0], pieces[1])
    pieces = narrow_sum(pieces[0], *[shift(pieces[k], k) for k in (2, 1, 3)])
    pieces = [pieces[0]] + [near_swap(pieces[k], k) for k in (1, 2, 3)]

    parts = exchange(partial_first.reshape(n_dp, rows_a, half), SAMPLES)
    parts = jnp.sum(parts.reshape(n_dp // 2, 2, rows_a, half).astype(F32), axis=0).astype(BF16)
    first_view_gradient = jnp.concatenate([parts[0], parts[1]], axis=1)
    first_view_gradient, *pieces = lax.optimization_barrier([first_view_gradient] + pieces)
    return first_view_gradient, narrow_sum(*pieces)


def solution(mesh):
    fine = Mesh(
        mesh.devices.reshape(4, 4, 2, 2, 4, 2), ("zh", "yk", "yl", "zl", "x", "core")
    )
    specs = (P(SAMPLES, FEATURES), P(FEATURES, SAMPLES))
    return jax.shard_map(
        shards, mesh=fine, in_specs=specs, out_specs=specs, check_vma=False
    )
```
